512 devices in a mesh: seq: 16 (over y_hi, z), res: 32 (over x, y_lo, core).
Axes of the slice: x: 4, y: 8 (y_hi: 2, y_lo: 4; y = y_hi * 4 + y_lo), z: 8, core: 2. Of those that a mesh axis runs over, the one named last changes fastest.
Arguments:
- homolog_matrix: bfloat16 [32, 2048, 256], P('seq', 'res'), may hold values from -6 to 6
- factor_matrix: bfloat16 [256, 64], replicated, may hold values from -0.375 to 0.375
- output_weight: bfloat16 [1024, 128], replicated, may hold values from -1.5 to 1.5
- output_bias: float32 [128], replicated, may hold values from -3 to 3
- pairwise_cotangent: bfloat16 [2048, 2048, 128], P('res', 'seq'), may hold values from -0.19921875 to 0.19921875
Outputs:
- pairwise_update: bfloat16 [2048, 2048, 128], P('res', 'seq')
- alignment_gradient: bfloat16 [32, 2048, 256], P('seq', 'res')
- factor_matrix_deriv: float32 [256, 64], replicated
- output_weight_gradient: float32 [1024, 128], replicated
The draws below stay inside these ranges and needn't reach their ends.
All inputs are finite; a program needn't handle non-finite values.
Results may differ from the reference program's by a relative error of at most 0.0073.
Values may be sent and summed in bfloat16 or wider, within the bound.
No kernel may reach another device: no remote copies, remote signals or barrier semaphores. Data moves between devices by JAX's collectives and lax.ppermute only.
A program may use at most 64 MiB of HBM per device.

```python
import jax
import jax.numpy as jnp
from jax import lax

FEATURE_WIDTH = 256
HIDDEN_WIDTH = 32
CZ = 128
HOMOLOG_TOTAL = 32
POSITION_TOTAL = 2048


def shard_levels(stream_key, extent, shards, smallest, largest):
    def one(dim, parts):
        heights = jax.random.uniform(jax.random.fold_in(jax.random.fold_in(stream_key, 6), dim), (parts,), jnp.float32, smallest / len(shards), largest / len(shards))
        return jnp.repeat(jnp.exp(heights), extent[dim] // parts).reshape((-1,) + (1,) * (len(extent) - dim - 1))

    gain = one(*shards[0])
    for cut in shards[1:]:
        gain = gain * one(*cut)
    return gain


def normal_values(rng, shape, spread, most, split=(), held_as=jnp.bfloat16):
    drawn = jax.random.normal(rng, shape, jnp.float32) * spread
    if len(split) > 0:
        drawn = shard_levels(rng, shape, split, -0.22, 0.18) * drawn
    return jnp.clip(drawn, min=-most, max=most).astype(held_as)


def setup_inputs(seed: int = 0) -> dict:
    arg_keys = jax.random.split(jax.random.key(seed), 6)
    homolog_matrix = normal_values(arg_keys[0], (HOMOLOG_TOTAL, POSITION_TOTAL, FEATURE_WIDTH), 1.0, 6.0, ((0, 16), (1, 32)))
    factor_matrix = normal_values(arg_keys[1], (FEATURE_WIDTH, 2 * HIDDEN_WIDTH), FEATURE_WIDTH ** -0.5, 0.375)
    output_weight = normal_values(arg_keys[2], (HIDDEN_WIDTH * HIDDEN_WIDTH, CZ), 0.25, 1.5)
    output_bias = normal_values(arg_keys[3], (CZ,), 0.5, 3.0, (), jnp.float32)
    pairwise_cotangent = normal_values(arg_keys[4], (POSITION_TOTAL, POSITION_TOTAL, CZ), 0.03125, 0.19921875, ((0, 32), (1, 16)))
    return {"homolog_matrix": homolog_matrix, "factor_matrix": factor_matrix, "output_weight": output_weight, "output_bias": output_bias, "pairwise_cotangent": pairwise_cotangent}


def layer_normalizer(values):
    center = lax.optimization_barrier(jnp.mean(values, axis=-1, keepdims=True))
    centered = values - center
    variance = lax.optimization_barrier(jnp.mean(centered * centered, axis=-1, keepdims=True))
    reciprocal_count = lax.rsqrt(variance + 1e-05)
    return (centered * reciprocal_count, reciprocal_count)

def reference(homolog_matrix, factor_matrix, output_weight, output_bias, pairwise_cotangent):
    inv_count = 1.0 / HOMOLOG_TOTAL
    normalized_alignment, reciprocal_count = layer_normalizer(homolog_matrix.astype(jnp.float32))
    standardized_reduced = normalized_alignment.astype(jnp.bfloat16)
    mapped_features = jnp.dot(standardized_reduced.reshape(-1, FEATURE_WIDTH), factor_matrix, preferred_element_type=jnp.float32)
    mapped_features = mapped_features.reshape(HOMOLOG_TOTAL, POSITION_TOTAL, 2 * HIDDEN_WIDTH)
    left_proj = mapped_features[:, :, :HIDDEN_WIDTH].astype(jnp.bfloat16)
    right_proj = mapped_features[:, :, HIDDEN_WIDTH:].astype(jnp.bfloat16)
    right_wide = right_proj.astype(jnp.float32)
    rows_per = min(16, POSITION_TOTAL)
    block_count = POSITION_TOTAL // rows_per

    def tile_step(totals, block_idx):
        wo_total, right_total = totals
        start = (block_idx * rows_per).astype(jnp.int32)
        left_block = lax.dynamic_slice_in_dim(left_proj, start, rows_per, 1).astype(jnp.float32)
        cot_block = lax.dynamic_slice_in_dim(pairwise_cotangent, start, rows_per, 0).reshape(-1, CZ)
        outer_sum = jnp.einsum('sic,sjd->ijcd', left_block, right_wide) * inv_count
        outer_low = outer_sum.reshape(-1, HIDDEN_WIDTH * HIDDEN_WIDTH).astype(jnp.bfloat16)
        pair_block = jnp.dot(outer_low, output_weight, preferred_element_type=jnp.float32) + output_bias
        pair_block = pair_block.astype(jnp.bfloat16).reshape(rows_per, POSITION_TOTAL, CZ)
        grad_outer = jnp.dot(cot_block, output_weight.T, preferred_element_type=jnp.float32).astype(jnp.bfloat16)
        wo_total = wo_total + jnp.dot(outer_low.T, cot_block, preferred_element_type=jnp.float32)
        grad_wide = grad_outer.astype(jnp.float32).reshape(rows_per, POSITION_TOTAL, HIDDEN_WIDTH, HIDDEN_WIDTH)
        left_terms = jnp.einsum('ijcd,sjd->sic', grad_wide, right_wide) * inv_count
        right_total = right_total + jnp.einsum('ijcd,sic->sjd', grad_wide, left_block) * inv_count
        return ((wo_total, right_total), (pair_block, left_terms))
    start_totals = (jnp.zeros((HIDDEN_WIDTH * HIDDEN_WIDTH, CZ), jnp.float32), jnp.zeros((HOMOLOG_TOTAL, POSITION_TOTAL, HIDDEN_WIDTH), jnp.float32))
    totals, stacked = lax.scan(tile_step, start_totals, jnp.arange(block_count, dtype=jnp.int32))
    output_weight_gradient, right_grad = totals
    pair_blocks, left_blocks = stacked
    pairwise_update = pair_blocks.reshape(POSITION_TOTAL, POSITION_TOTAL, CZ)
    left_grad = jnp.moveaxis(left_blocks, 0, 1).reshape(HOMOLOG_TOTAL, POSITION_TOTAL, HIDDEN_WIDTH)
    both_grads = jnp.concatenate([left_grad, right_grad], axis=-1).astype(jnp.bfloat16)
    raveled_derivs = both_grads.reshape(-1, 2 * HIDDEN_WIDTH)
    factor_matrix_deriv = jnp.dot(standardized_reduced.reshape(-1, FEATURE_WIDTH).T, raveled_derivs, preferred_element_type=jnp.float32)
    standardized_deriv = jnp.dot(raveled_derivs, factor_matrix.T, preferred_element_type=jnp.float32).reshape(HOMOLOG_TOTAL, POSITION_TOTAL, FEATURE_WIDTH)
    averaged_gradient = lax.optimization_barrier(jnp.mean(standardized_deriv, axis=-1, keepdims=True))
    averaged_outer = lax.optimization_barrier(jnp.mean(standardized_deriv * normalized_alignment, axis=-1, keepdims=True))
    alignment_gradient = (reciprocal_count * (standardized_deriv - averaged_gradient - normalized_alignment * averaged_outer)).astype(jnp.bfloat16)
    return (pairwise_update, alignment_gradient, factor_matrix_deriv, output_weight_gradient)
```

```python
import functools

import jax
import jax.numpy as jnp
from jax import lax
from jax.experimental import pallas as pl
from jax.experimental.pallas import tpu as pltpu
from jax.sharding import PartitionSpec as P

BF = jnp.bfloat16
F32 = jnp.float32
LANES = 128
VMEM_BYTES = 48 * 1024 * 1024
NN = (((1,), (0,)), ((), ()))
NT = (((1,), (1,)), ((), ()))


def dot(a, b, dims=NN):
    return lax.dot_general(a, b, dims, preferred_element_type=F32)


def params():
    return pltpu.CompilerParams(vmem_limit_bytes=VMEM_BYTES)


def whole(shape):
    return pl.BlockSpec(shape, lambda *_: (0,) * len(shape))


def low_lanes(shape, width):
    return lax.broadcasted_iota(jnp.int32, shape, len(shape) - 1) < width


def wide_cotangent(cot_ref):
    return jnp.concatenate([cot_ref[i] for i in range(cot_ref.shape[0])], axis=1)


def left_rows_kernel(recv_ref, spread, rows_ref, inv_count):
    nq, width, lanes = recv_ref.shape
    per = lanes // width
    residues = lanes // 2
    for high in range(nq // per):
        block = recv_ref[high * per : (high + 1) * per].reshape(lanes, lanes).astype(F32)
        turned = block.T * inv_count
        for low in range(per):
            shift = (lanes - low * width) % lanes
            part = turned if shift == 0 else pltpu.roll(turned, shift, 1)
            spread[pl.ds((high * per + low) * lanes, lanes), :] = part

    def one(i, carry):
        for s in range(2):
            part = spread[pl.ds(s * residues + i, nq, stride=lanes), :].astype(BF)
            rows_ref[pl.ds(pl.multiple_of((i * 2 + s) * nq, nq), nq), :] = part
        return carry

    lax.fori_loop(0, residues, one, 0, unroll=8)


def first_kernel(inv_count, recv_ref, w_ref, cot_ref, q_ref, rows_ref, out_ref, spread, acc):
    step = pl.program_id(0)
    block = cot_ref.shape[0]
    nq, width, lanes = recv_ref.shape
    seqs = 2 * nq

    @pl.when(step == 0)
    def _():
        left_rows_kernel(recv_ref, spread, rows_ref, inv_count)

    rows = rows_ref[pl.ds(pl.multiple_of(step * block * seqs, block * seqs), block * seqs), :][:, :width]
    pair = 2 * lanes
    for n in range(w_ref.shape[1] // pair):
        piece = dot(rows, w_ref[:, n * pair : (n + 1) * pair]).astype(BF)
        for k in range(2):
            d = n * 2 + k
            for i in range(block):
                q_ref[0, d * seqs : (d + 1) * seqs, i * lanes : (i + 1) * lanes] = piece[
                    i * seqs : (i + 1) * seqs, k * lanes : (k + 1) * lanes
                ]
    cot = wide_cotangent(cot_ref)
    part = dot(q_ref[0], cot, NT)

    @pl.when(step == 0)
    def _():
        acc[...] = part

    @pl.when(step > 0)
    def _():
        acc[...] += part

    @pl.when(step == pl.num_programs(0) - 1)
    def _():
        low = low_lanes((width, lanes), lanes // 2)
        for q in range(nq):
            a = acc[pl.ds(q, width, stride=seqs), :]
            b = acc[pl.ds(nq + q, width, stride=seqs), :]
            out_ref[2 * q] = jnp.where(low, a, pltpu.roll(b, lanes // 2, 1)).astype(BF)
            out_ref[2 * q + 1] = jnp.where(low, pltpu.roll(a, lanes // 2, 1), b).astype(BF)


def first(recv, w, cot, inv_count, block=8):
    nq, width, lanes = recv.shape
    residues, cols, ch = cot.shape
    seqs = 2 * nq
    steps = residues // block
    return pl.pallas_call(
        functools.partial(first_kernel, inv_count),
        grid=(steps,),
        in_specs=[
            whole(recv.shape),
            whole(w.shape),
            pl.BlockSpec((block, cols, ch), lambda s: (s, 0, 0)),
        ],
        out_specs=[
            pl.BlockSpec((1, width * seqs, block * ch), lambda s: (s, 0, 0)),
            whole((residues * seqs, lanes)),
            whole((2 * nq, width, lanes)),
        ],
        out_shape=[
            jax.ShapeDtypeStruct((steps, width * seqs, block * ch), BF),
            jax.ShapeDtypeStruct((residues * seqs, lanes), BF),
            jax.ShapeDtypeStruct((2 * nq, width, lanes), BF),
        ],
        scratch_shapes=[
            pltpu.VMEM((nq * lanes, lanes), F32),
            pltpu.VMEM((width * seqs, cols), F32),
        ],
        compiler_params=params(),
        cost_estimate=pl.CostEstimate(flops=40_000_000_000, bytes_accessed=20_000_000, transcendentals=0),
        name="first",
    )(recv, w, cot)


def second_kernel(inv_count, recv_ref, w_ref, cot_ref, h_ref, rt_ref, out_ref, spread, left):
    step = pl.program_id(0)
    block = cot_ref.shape[0]
    nr, width, lanes = recv_ref.shape
    nq = nr // 2
    seqs = 2 * nq
    residues = left.shape[0] // seqs

    @pl.when(step == 0)
    def _():
        spread[...] = recv_ref[...].reshape(nr * width, lanes).astype(F32)
        low = low_lanes((nq, lanes), lanes // 2)
        for d in range(width):
            a = spread[pl.ds(d, nq, stride=2 * width), :]
            b = spread[pl.ds(width + d, nq, stride=2 * width), :]
            rt_ref[(2 * d) * nq : (2 * d + 1) * nq, :] = jnp.where(low, a, pltpu.roll(b, lanes // 2, 1)).astype(BF)
            rt_ref[(2 * d + 1) * nq : (2 * d + 2) * nq, :] = jnp.where(low, pltpu.roll(a, lanes // 2, 1), b).astype(BF)

    cot = wide_cotangent(cot_ref)
    group = 8
    for m in range(width // group):
        mine = rt_ref[m * group * seqs : (m + 1) * group * seqs, :]
        for n in range(block // 2):
            piece = dot(mine, cot[:, n * 2 * lanes : (n + 1) * 2 * lanes]).astype(BF)
            for g in range(group):
                d = m * group + g
                for k in range(2):
                    i = 2 * n + k
                    h_ref[i * seqs : (i + 1) * seqs, d * lanes : (d + 1) * lanes] = piece[
                        g * seqs : (g + 1) * seqs, k * lanes : (k + 1) * lanes
                    ]
    start = pl.multiple_of(step * block * seqs, block * seqs)
    left[pl.ds(start, block * seqs), :width] = dot(h_ref[...], w_ref[...], NT) * inv_count

    @pl.when(step == pl.num_programs(0) - 1)
    def _():
        per = lanes // width
        lane = lax.broadcasted_iota(jnp.int32, (lanes, lanes), 1)
        for high in range(nq // per):
            total = None
            for low in range(per):
                q = high * per + low
                part = jnp.concatenate(
                    [left[pl.ds(s * nq + q, residues, stride=seqs), :] for s in range(2)], axis=0
                )
                if low == 0:
                    total = part
                else:
                    total = jnp.where(lane < low * width, total, pltpu.roll(part, low * width, 1))
            out_ref[high * per : (high + 1) * per] = total.T.astype(BF).reshape(per, width, lanes)


def second(recv, w, cot, inv_count, block=8):
    nr, width, lanes = recv.shape
    residues, cols, ch = cot.shape
    nq = nr // 2
    seqs = 2 * nq
    steps = residues // block
    return pl.pallas_call(
        functools.partial(second_kernel, inv_count),
        grid=(steps,),
        in_specs=[
            whole(recv.shape),
            whole(w.shape),
            pl.BlockSpec((block, cols, ch), lambda s: (s, 0, 0)),
        ],
        out_specs=[
            pl.BlockSpec((block * seqs, width * ch), lambda s: (s, 0)),
            whole((width * seqs, cols)),
            whole((nq, width, lanes)),
        ],
        out_shape=[
            jax.ShapeDtypeStruct((residues * seqs, width * ch), BF),
            jax.ShapeDtypeStruct((width * seqs, cols), BF),
            jax.ShapeDtypeStruct((nq, width, lanes), BF),
        ],
        scratch_shapes=[
            pltpu.VMEM((nr * width, lanes), F32),
            pltpu.VMEM((residues * seqs, lanes), F32),
        ],
        compiler_params=params(),
        cost_estimate=pl.CostEstimate(flops=40_000_000_000, bytes_accessed=20_000_000, transcendentals=0),
        name="second",
    )(recv, w, cot)


def third_kernel(rows_ref, h_ref, out_ref, turned):
    @pl.when(pl.program_id(0) == 0)
    def _():
        rows = rows_ref.shape[0]
        for k in range(rows // LANES):
            part = rows_ref[k * LANES : (k + 1) * LANES, :].astype(F32).T
            turned[:, k * LANES : (k + 1) * LANES] = part[: turned.shape[0]].astype(BF)

    total = dot(turned[...], h_ref[...])
    for d in range(out_ref.shape[0]):
        out_ref[d] = total[:, d * LANES : (d + 1) * LANES].astype(BF)


def third(rows, h, width, block=1024):
    count, wide = h.shape
    return pl.pallas_call(
        third_kernel,
        grid=(wide // block,),
        in_specs=[whole(rows.shape), pl.BlockSpec((count, block), lambda s: (0, s))],
        out_specs=pl.BlockSpec((block // LANES, width, LANES), lambda s: (s, 0, 0)),
        out_shape=jax.ShapeDtypeStruct((wide // LANES, width, LANES), BF),
        scratch_shapes=[pltpu.VMEM((width, count), BF)],
        compiler_params=params(),
        cost_estimate=pl.CostEstimate(flops=20_000_000_000, bytes_accessed=17_000_000, transcendentals=0),
        name="third",
    )(rows, h)


def fourth_kernel(rt_ref, q_ref, bias_ref, out_ref, r):
    @pl.when(pl.program_id(0) == 0)
    def _():
        for k in range(rt_ref.shape[0] // LANES):
            r[:, k * LANES : (k + 1) * LANES] = rt_ref[k * LANES : (k + 1) * LANES, :].astype(F32).T.astype(BF)

    bias = bias_ref[...]
    mine = r[...]
    for n in range(out_ref.shape[0] // 2):
        piece = dot(mine, q_ref[0, :, n * 2 * LANES : (n + 1) * 2 * LANES])
        for k in range(2):
            out_ref[2 * n + k] = (piece[:, k * LANES : (k + 1) * LANES] + bias).astype(BF)


def fourth(rt, q, bias):
    steps, depth, wide = q.shape
    cols = rt.shape[1]
    ch = bias.shape[1]
    block = wide // ch
    return pl.pallas_call(
        fourth_kernel,
        grid=(steps,),
        in_specs=[whole(rt.shape), pl.BlockSpec((1, depth, wide), lambda s: (s, 0, 0)), whole(bias.shape)],
        out_specs=pl.BlockSpec((block, cols, ch), lambda s: (s, 0, 0)),
        out_shape=jax.ShapeDtypeStruct((steps * block, cols, ch), BF),
        scratch_shapes=[pltpu.VMEM((cols, depth), BF)],
        compiler_params=params(),
        cost_estimate=pl.CostEstimate(flops=20_000_000_000, bytes_accessed=19_000_000, transcendentals=0),
        name="fourth",
    )(rt, q, bias)


def before_kernel(x_ref, factor_ref, left_ref, right_ref):
    low_normed = standardize(x_ref)[0].astype(BF)
    mapped = dot(low_normed, factor_ref[...])
    width = mapped.shape[1] // 2
    padded = jnp.concatenate([mapped, jnp.zeros((mapped.shape[0], LANES - 2 * width), F32)], axis=1)
    turned = padded.T.astype(BF)
    for q in range(left_ref.shape[0]):
        left_ref[q] = turned[:width]
    right_ref[...] = turned[width : 2 * width]


def standardize(x_ref):
    seqs, residues, ch = x_ref.shape
    x = x_ref[...].reshape(seqs * residues, ch).astype(F32)
    centered = x - jnp.mean(x, axis=-1, keepdims=True)
    variance = jnp.mean(centered * centered, axis=-1, keepdims=True)
    scale = lax.rsqrt(variance + 1e-05)
    return centered * scale, scale


def before(x, factor, copies):
    width = factor.shape[1] // 2
    rows = x.shape[0] * x.shape[1]
    return pl.pallas_call(
        before_kernel,
        out_shape=[
            jax.ShapeDtypeStruct((copies, width, rows), BF),
            jax.ShapeDtypeStruct((width, rows), BF),
        ],
        compiler_params=params(),
        name="before",
    )(x, factor)


def after_kernel(left_ref, right_ref, x_ref, factor_ref, wo_ref, grad_ref, out_ref):
    left = jnp.sum(left_ref[...].astype(F32), axis=0)
    both = jnp.concatenate([left, right_ref[...]], axis=0)
    rows = both.shape[1]
    low_both = both.astype(BF)
    normed, scale = standardize(x_ref)
    factor_part = dot(low_both, normed.astype(BF))
    padded = jnp.concatenate([both, jnp.zeros((LANES - both.shape[0], rows), F32)], axis=0)
    turned = padded.T[:, : both.shape[0]].astype(BF)
    deriv = dot(turned, factor_ref[...], NT)
    mean = jnp.mean(deriv, axis=-1, keepdims=True)
    along = jnp.mean(deriv * normed, axis=-1, keepdims=True)
    grad_ref[...] = (scale * (deriv - mean - normed * along)).astype(BF).reshape(grad_ref.shape)
    chunks, width, _ = wo_ref.shape
    extra = out_ref.shape[1] - width
    out_ref[:, :width, :] = wo_ref[...]
    out_ref[:, width:, :] = jnp.zeros((chunks, extra, LANES), BF)
    stacked = jnp.concatenate(
        [factor_part[:, k * LANES : (k + 1) * LANES] for k in range(factor_part.shape[1] // LANES)], axis=0
    ).astype(BF)
    for k in range(stacked.shape[0] // extra):
        out_ref[k, width:, :] = stacked[k * extra : (k + 1) * extra]


def after(left, right, x, factor, wo):
    chunks, width, lanes = wo.shape
    return pl.pallas_call(
        after_kernel,
        out_shape=[
            jax.ShapeDtypeStruct(x.shape, BF),
            jax.ShapeDtypeStruct((chunks, width + 16, lanes), BF),
        ],
        compiler_params=params(),
        name="after",
    )(left, right, x, factor, wo)


def total_kernel(in_ref, out_ref):
    out_ref[...] = jnp.sum(in_ref[...].astype(F32), axis=0)


def total(parts):
    return pl.pallas_call(
        total_kernel,
        out_shape=jax.ShapeDtypeStruct(parts.shape[1:], F32),
        compiler_params=params(),
        name="total",
    )(parts)


def total_copies_kernel(in_ref, out_ref):
    summed = jnp.sum(in_ref[...].astype(F32), axis=0).astype(BF)
    for k in range(out_ref.shape[0]):
        out_ref[k] = summed


def total_copies(parts, copies):
    return pl.pallas_call(
        total_copies_kernel,
        out_shape=jax.ShapeDtypeStruct((copies,) + parts.shape[1:], BF),
        compiler_params=params(),
        name="total_copies",
    )(parts)


def last_kernel(in_ref, factor_ref, weight_ref):
    chunks, tall, lanes = in_ref.shape
    extra = 16
    width = tall - extra
    for d in range(chunks):
        weight_ref[pl.ds(d, width, stride=chunks), :] = in_ref[d, :width, :].astype(F32)
    ch, both = factor_ref.shape
    used = ch * both // (lanes * extra)
    stacked = in_ref[:used, width:, :].reshape(used * extra, lanes).astype(F32)
    halves = ch // lanes
    for k in range(halves):
        part = stacked[k * both : (k + 1) * both]
        padded = jnp.concatenate([part, jnp.zeros((lanes - both, lanes), F32)], axis=0)
        factor_ref[k * lanes : (k + 1) * lanes, :] = padded.T[:, :both]


def last(parts, factor_shape):
    chunks, tall, lanes = parts.shape
    return pl.pallas_call(
        last_kernel,
        out_shape=[
            jax.ShapeDtypeStruct(factor_shape, F32),
            jax.ShapeDtypeStruct((chunks * (tall - 16), lanes), F32),
        ],
        compiler_params=params(),
        name="last",
    )(parts)


def exchange(parts, axis):
    return lax.all_to_all(parts, axis, 0, 0, tiled=True)


def body(nq, nr, homolog_matrix, factor_matrix, output_weight, output_bias, pairwise_cotangent):
    width = factor_matrix.shape[1] // 2
    inv_count = 1.0 / (2 * nq)
    there = [(s * nr + r, (r // 2) * nr + 2 * s + r % 2) for s in range(nq) for r in range(nr)]
    back = [(b, a) for a, b in there]
    w = output_weight.reshape(width, -1)
    bias = output_bias.reshape(1, -1)
    left_parts, right_mine = before(homolog_matrix, factor_matrix, nq)
    right_moved = lax.ppermute(right_mine, ("seq", "res"), there)
    left_all = exchange(left_parts, "seq")
    right_all = exchange(jnp.broadcast_to(right_moved, (nr,) + right_moved.shape), "res")
    q, rows, right_out = first(left_all, w, pairwise_cotangent, inv_count)
    right_in = exchange(right_out, "res")
    h, rt, left_out = second(right_all, w, pairwise_cotangent, inv_count)
    left_in = exchange(left_out, "seq")
    wo = third(rows, h, width)
    pairwise_update = fourth(rt, q, bias)
    right_total = lax.ppermute(total(right_in), ("seq", "res"), back)
    alignment_gradient, payload = after(left_in, right_total, homolog_matrix, factor_matrix, wo)
    summed = total_copies(exchange(payload, "res"), nq)
    summed = total_copies(exchange(summed, "seq"), nr)
    factor_matrix_deriv, output_weight_gradient = last(exchange(summed, "res"), factor_matrix.shape)
    return (pairwise_update, alignment_gradient, factor_matrix_deriv, output_weight_gradient)


def solution(mesh):
    placed = (P("seq", "res", None), P(), P(), P(), P("res", "seq", None))
    return jax.shard_map(
        functools.partial(body, mesh.shape["seq"], mesh.shape["res"]),
        mesh=mesh,
        in_specs=placed,
        out_specs=(P("res", "seq", None), P("seq", "res", None), P(), P()),
        check_vma=False,
    )
```

```python
import functools

import jax
import jax.numpy as jnp
from jax import lax
from jax.experimental import pallas as pl
from jax.experimental.pallas import tpu as pltpu
from jax.sharding import PartitionSpec as P

BF = jnp.bfloat16
F32 = jnp.float32
LANES = 128
MIB = 1024 * 1024
BIG = 56
NN = (((1,), (0,)), ((), ()))
NT = (((1,), (1,)), ((), ()))


def dot(a, b, dims=NN):
    return lax.dot_general(a, b, dims, preferred_element_type=F32)


def params(size=16):
    return pltpu.CompilerParams(vmem_limit_bytes=size * MIB)


def whole(shape):
    return pl.BlockSpec(shape, lambda *_: (0,) * len(shape))


def low_lanes(shape, width):
    return lax.broadcasted_iota(jnp.int32, shape, len(shape) - 1) < width


def cost(flops):
    return pl.CostEstimate(flops=flops, bytes_accessed=4_000_000, transcendentals=0)


def standardize(x_ref):
    seqs, residues, ch = x_ref.shape
    x = x_ref[...].reshape(seqs * residues, ch).astype(F32)
    centered = x - jnp.mean(x, axis=-1, keepdims=True)
    variance = jnp.mean(centered * centered, axis=-1, keepdims=True)
    scale = lax.rsqrt(variance + 1e-05)
    return centered * scale, scale


def before_kernel(x_ref, factor_ref, left_ref, packed_ref, held):
    normed = standardize(x_ref)[0].astype(BF)
    packed_ref[: normed.shape[0], :] = normed
    mapped = dot(normed, factor_ref[...], NT)
    rows, both = mapped.shape
    width = both // 2
    per = LANES // width
    padded = jnp.concatenate([mapped, jnp.zeros((rows, LANES - both), F32)], axis=1)
    turned = padded.T[width:both].astype(BF)
    parts = normed.shape[1] // LANES
    few = width // parts
    packed_ref[normed.shape[0] :, :] = jnp.concatenate([turned[k * few : (k + 1) * few] for k in range(parts)], axis=1)
    held[...] = padded
    lane = lax.broadcasted_iota(jnp.int32, (rows // per, LANES), 1)
    total = held[pl.ds(0, rows // per, stride=per), :]
    for low in range(1, per):
        part = pltpu.roll(held[pl.ds(low, rows // per, stride=per), :], low * width, 1)
        total = jnp.where(lane < low * width, total, part)
    left_ref[...] = total.astype(BF)


def before(x, factor):
    width = factor.shape[0] // 2
    rows = x.shape[0] * x.shape[1]
    return pl.pallas_call(
        before_kernel,
        out_shape=[
            jax.ShapeDtypeStruct((rows * width // LANES, LANES), BF),
            jax.ShapeDtypeStruct((rows + width * rows // x.shape[2], x.shape[2]), BF),
        ],
        scratch_shapes=[pltpu.VMEM((rows, LANES), F32)],
        compiler_params=params(BIG),
        name="before",
    )(x, factor)


def rows_of(ref, index, count):
    return ref.at[pl.ds(pl.multiple_of(index * count, count), count), :]


def grad_outer_kernel(parts, given_ref, cot_ref, out_ref, w_ref, wide, held, sems):
    residues, cols, ch = cot_ref.shape
    block = residues // parts
    count = out_ref.shape[0] // parts
    width = count // block
    group = LANES // width
    wide[...] = given_ref[...].astype(F32)
    depth = wide.shape[0] // width
    for d in range(depth):
        w_ref[d * width : (d + 1) * width, :] = wide[pl.ds(d, width, stride=depth), :].astype(BF)

    def copy(index):
        return pltpu.make_async_copy(rows_of(held, index, count), rows_of(out_ref, index, count), sems.at[index])

    def one(index, carry):
        for n in range(block // 2):
            cot = cot_ref[pl.ds(index * block + 2 * n, 2)].reshape(2 * cols, ch)
            for m in range(w_ref.shape[0] // LANES):
                piece = dot(w_ref[m * LANES : (m + 1) * LANES, :], cot, NT).astype(BF)
                for k in range(2):
                    row = pl.multiple_of(index * count + (2 * n + k) * width, width)
                    for g in range(group):
                        d = m * group + g
                        held[pl.ds(row, width), d * cols : (d + 1) * cols] = piece[
                            g * width : (g + 1) * width, k * cols : (k + 1) * cols
                        ]
        copy(index).start()
        return carry

    lax.fori_loop(0, parts, one, 0)
    lax.fori_loop(0, parts, lambda index, carry: copy(index).wait(), None)


def grad_outer(w, cot, width, parts=8):
    residues, cols, ch = cot.shape
    shape = (residues * width, w.shape[0] // width * cols)
    return pl.pallas_call(
        functools.partial(grad_outer_kernel, parts),
        in_specs=[whole(w.shape), whole(cot.shape)],
        out_specs=[pl.BlockSpec(memory_space=pl.ANY), whole(w.shape)],
        grid=(1,),
        out_shape=[jax.ShapeDtypeStruct(shape, BF), jax.ShapeDtypeStruct(w.shape, BF)],
        scratch_shapes=[pltpu.VMEM(w.shape, F32), pltpu.VMEM(shape, BF), pltpu.SemaphoreType.DMA((parts,))],
        compiler_params=params(BIG),
        cost_estimate=cost(8_000_000_000),
        name="grad_outer",
    )(w, cot)


def right_kernel(inv_count, parts, recv_ref, grad_ref, out_ref, held, sems, spread, rows, sums, totals):
    nq, tall, lanes = recv_ref.shape
    width = out_ref.shape[1]
    count = grad_ref.shape[0] // parts
    half = lanes // 2

    def copy(index):
        return pltpu.make_async_copy(rows_of(grad_ref, index, count), rows_of(held, index, count), sems.at[index])

    lax.fori_loop(0, parts, lambda index, carry: copy(index).start(), None)
    spread[...] = recv_ref[...].reshape(nq * tall, lanes).astype(F32) * inv_count
    for s in range(2):
        for t in range(tall // 2):
            rows[t * lanes // count, s * nq : (s + 1) * nq, t * lanes % count : t * lanes % count + lanes] = spread[
                pl.ds(s * (tall // 2) + t, nq, stride=tall), :
            ].astype(BF)
    sums[...] = jnp.zeros_like(sums)

    def one(index, carry):
        copy(index).wait()
        sums[...] += dot(rows[index], rows_of(held, index, count)[...])
        return carry

    lax.fori_loop(0, parts, one, 0)
    low = low_lanes((nq, lanes), half)
    for d in range(width):
        a = sums[:nq, d * lanes : (d + 1) * lanes]
        b = sums[nq:, d * lanes : (d + 1) * lanes]
        totals[pl.ds(d, nq, stride=2 * width), :] = jnp.where(low, a, pltpu.roll(b, half, 1))
        totals[pl.ds(width + d, nq, stride=2 * width), :] = jnp.where(low, pltpu.roll(a, half, 1), b)
    out_ref[...] = totals[...].reshape(out_ref.shape).astype(BF)


def right(recv, grad, width, inv_count, parts=8):
    nq, tall, lanes = recv.shape
    depth, wide = grad.shape
    out = (2 * nq, width, lanes)
    return pl.pallas_call(
        functools.partial(right_kernel, inv_count, parts),
        in_specs=[whole(recv.shape), pl.BlockSpec(memory_space=pl.ANY)],
        out_specs=whole(out),
        grid=(1,),
        out_shape=jax.ShapeDtypeStruct(out, BF),
        scratch_shapes=[
            pltpu.VMEM(grad.shape, BF),
            pltpu.SemaphoreType.DMA((parts,)),
            pltpu.VMEM((nq * tall, lanes), F32),
            pltpu.VMEM((parts, 2 * nq, depth // parts), BF),
            pltpu.VMEM((2 * nq, wide), F32),
            pltpu.VMEM((2 * nq * width, lanes), F32),
        ],
        compiler_params=params(BIG),
        cost_estimate=cost(8_000_000_000),
        name="right",
    )(recv, grad)


def left_kernel(inv_count, parts, recv_ref, grad_ref, rt_ref, out_ref, held, sems, spread, rows, totals):
    nr, width, lanes = recv_ref.shape
    nq = nr // 2
    tall = out_ref.shape[1]
    count = grad_ref.shape[0] // parts

    def copy(index):
        return pltpu.make_async_copy(rows_of(grad_ref, index, count), rows_of(held, index, count), sems.at[index])

    lax.fori_loop(0, parts, lambda index, carry: copy(index).start(), None)
    spread[...] = recv_ref[...].reshape(nr * width, lanes).astype(F32)
    low = low_lanes((nq, lanes), lanes // 2)
    for d in range(width):
        a = spread[pl.ds(d, nq, stride=2 * width), :]
        b = spread[pl.ds(width + d, nq, stride=2 * width), :]
        first = jnp.where(low, a, pltpu.roll(b, lanes // 2, 1)).astype(BF)
        second = jnp.where(low, pltpu.roll(a, lanes // 2, 1), b).astype(BF)
        rt_ref[(2 * d) * nq : (2 * d + 1) * nq, :] = first
        rt_ref[(2 * d + 1) * nq : (2 * d + 2) * nq, :] = second
        rows[:nq, d * lanes : (d + 1) * lanes] = first
        rows[nq:, d * lanes : (d + 1) * lanes] = second

    def one(index, carry):
        copy(index).wait()
        part = dot(rows[...], rows_of(held, index, count)[...], NT) * inv_count
        for k in range(count // lanes):
            for s in range(2):
                t = s * (tall // 2) + index * (count // lanes) + k
                totals[pl.ds(t, nq, stride=tall), :] = part[s * nq : (s + 1) * nq, k * lanes : (k + 1) * lanes]
        return carry

    lax.fori_loop(0, parts, one, 0)
    out_ref[...] = totals[...].reshape(out_ref.shape).astype(BF)


def left(recv, grad, inv_count, parts=8):
    nr, width, lanes = recv.shape
    nq = nr // 2
    deep, wide = grad.shape
    out = (nq, 2 * deep // lanes, lanes)
    return pl.pallas_call(
        functools.partial(left_kernel, inv_count, parts),
        in_specs=[whole(recv.shape), pl.BlockSpec(memory_space=pl.ANY)],
        out_specs=[whole((nr * width, lanes)), whole(out)],
        grid=(1,),
        out_shape=[jax.ShapeDtypeStruct((nr * width, lanes), BF), jax.ShapeDtypeStruct(out, BF)],
        scratch_shapes=[
            pltpu.VMEM(grad.shape, BF),
            pltpu.SemaphoreType.DMA((parts,)),
            pltpu.VMEM((nr * width, lanes), F32),
            pltpu.VMEM((nr, wide), BF),
            pltpu.VMEM((out[0] * out[1], lanes), F32),
        ],
        compiler_params=params(BIG),
        cost_estimate=cost(8_000_000_000),
        name="left",
    )(recv, grad)


def weight_kernel(inv_count, recv_ref, rt_ref, cot_ref, out_ref, rows_ref, spread, held, totals):
    step = pl.program_id(0)
    nq, tall, lanes = recv_ref.shape
    block, cols, ch = cot_ref.shape
    depth, width, _ = out_ref.shape
    seqs = 2 * nq
    group = lanes // seqs

    @pl.when(step == 0)
    def _():
        per = lanes // width
        spread[...] = recv_ref[...].reshape(nq * tall, lanes).astype(F32) * inv_count
        for t in range(tall // 2):
            for s in range(2):
                part = spread[pl.ds(s * (tall // 2) + t, nq, stride=tall), :]
                for low in range(per):
                    mine = part if low == 0 else pltpu.roll(part, lanes - low * width, 1)
                    row = ((t * per + low) * 2 + s) * nq
                    rows_ref[row : row + nq, :] = mine.astype(BF)

    cot = jnp.concatenate([cot_ref[i] for i in range(block)], axis=1)
    for m in range(depth // group):
        mine = rt_ref[m * lanes : (m + 1) * lanes, :]
        for n in range(block // 2):
            piece = dot(mine, cot[:, n * 2 * ch : (n + 1) * 2 * ch]).astype(BF)
            for g in range(group):
                d = m * group + g
                for k in range(2):
                    i = 2 * n + k
                    held[i * seqs : (i + 1) * seqs, d * ch : (d + 1) * ch] = piece[
                        g * seqs : (g + 1) * seqs, k * ch : (k + 1) * ch
                    ]
    count = block * seqs
    start = pl.multiple_of(step * count, count)
    turned = jnp.concatenate(
        [
            rows_ref[pl.ds(start + k * lanes, lanes), :].astype(F32).T[:width].astype(BF)
            for k in range(count // lanes)
        ],
        axis=1,
    )
    part = dot(turned, held[...])

    @pl.when(step == 0)
    def _():
        totals[...] = part

    @pl.when(step > 0)
    def _():
        totals[...] += part

    @pl.when(step == pl.num_programs(0) - 1)
    def _():
        for d in range(depth):
            out_ref[d] = totals[:, d * ch : (d + 1) * ch].astype(BF)


def weight(recv, rt, cot, width, inv_count, block=8):
    nq, tall, lanes = recv.shape
    residues, cols, ch = cot.shape
    seqs = 2 * nq
    depth = rt.shape[0] // seqs
    out = (depth, width, ch)
    return pl.pallas_call(
        functools.partial(weight_kernel, inv_count),
        grid=(residues // block,),
        in_specs=[whole(recv.shape), whole(rt.shape), pl.BlockSpec((block, cols, ch), lambda s: (s, 0, 0))],
        out_specs=[whole(out), whole((residues * seqs, lanes))],
        out_shape=[jax.ShapeDtypeStruct(out, BF), jax.ShapeDtypeStruct((residues * seqs, lanes), BF)],
        scratch_shapes=[
            pltpu.VMEM((nq * tall, lanes), F32),
            pltpu.VMEM((block * seqs, depth * ch), BF),
            pltpu.VMEM((width, depth * ch), F32),
        ],
        compiler_params=params(BIG),
        cost_estimate=cost(16_000_000_000),
        name="weight",
    )(recv, rt, cot)


def pair_kernel(rows_ref, w_ref, rt_ref, bias_ref, *refs):
    out_ref, token_ref, r, held = refs[-4:]
    block, cols, ch = out_ref.shape
    depth = held.shape[0]
    seqs = rows_ref.shape[0] // block
    width = w_ref.shape[0] * seqs // depth

    @pl.when(pl.program_id(0) == 0)
    def _():
        token_ref[...] = jnp.zeros_like(token_ref)
        for k in range(depth // LANES):
            r[:, k * LANES : (k + 1) * LANES] = rt_ref[k * LANES : (k + 1) * LANES, :].astype(F32).T.astype(BF)

    rows = rows_ref[:, :width]
    for n in range(depth // seqs // 2):
        w = jnp.concatenate([w_ref[(2 * n + k) * width : (2 * n + k + 1) * width, :] for k in range(2)], axis=1)
        piece = dot(rows, w).astype(BF)
        for k in range(2):
            d = 2 * n + k
            for i in range(block):
                held[d * seqs : (d + 1) * seqs, i * ch : (i + 1) * ch] = piece[
                    i * seqs : (i + 1) * seqs, k * ch : (k + 1) * ch
                ]
    bias = bias_ref[...]
    mine = r[...]
    for n in range(block // 2):
        piece = dot(mine, held[:, n * 2 * ch : (n + 1) * 2 * ch])
        for k in range(2):
            out_ref[2 * n + k] = (piece[:, k * ch : (k + 1) * ch] + bias).astype(BF)


def pair_part(rows, w, rt, bias, residues, begin, end, behind, held=None, block=8):
    count, lanes = rows.shape
    seqs = count // residues
    depth, cols = rt.shape
    ch = bias.shape[1]
    anywhere = pl.BlockSpec(memory_space=pl.ANY)
    more = [behind] + ([] if held is None else [held])
    return pl.pallas_call(
        pair_kernel,
        grid=(end - begin,),
        in_specs=[
            pl.BlockSpec((block * seqs, lanes), lambda s: (s + begin, 0)),
            whole(w.shape),
            whole(rt.shape),
            whole(bias.shape),
        ]
        + [anywhere] * len(more),
        out_specs=[pl.BlockSpec((block, cols, ch), lambda s: (s + begin, 0, 0)), whole((8, LANES))],
        out_shape=[
            jax.ShapeDtypeStruct((residues, cols, ch), BF),
            jax.ShapeDtypeStruct((8, LANES), F32),
        ],
        scratch_shapes=[pltpu.VMEM((cols, depth), BF), pltpu.VMEM((depth, block * ch), BF)],
        input_output_aliases={} if held is None else {5: 0},
        compiler_params=params(BIG),
        cost_estimate=cost(6_000_000_000),
        name="pair_part",
    )(rows, w, rt, bias, *more)


def left_rows(left_ref, held):
    added = jnp.sum(left_ref[...].astype(F32), axis=0)
    per = held.shape[0] // added.shape[0]
    width = LANES // per
    for low in range(per):
        part = added if low == 0 else pltpu.roll(added, LANES - low * width, 1)
        held[pl.ds(low, added.shape[0], stride=per), :] = part


def payload_kernel(left_ref, right_ref, normed_ref, moved_ref, wo_ref, out_ref, held):
    left_rows(left_ref, held)
    chunks, width, _ = wo_ref.shape
    left_grad = held[...].T[:width].astype(BF)
    factor_part = jnp.concatenate(
        [dot(left_grad, normed_ref[: held.shape[0], :]), dot(right_ref[...].astype(BF), moved_ref[: held.shape[0], :])], axis=0
    )
    stacked = jnp.concatenate(
        [factor_part[:, k * LANES : (k + 1) * LANES] for k in range(factor_part.shape[1] // LANES)], axis=0
    )
    coarse = stacked.astype(BF)
    fine = (stacked - coarse.astype(F32)).astype(BF)
    rows = stacked.shape[0] // chunks
    for k in range(chunks):
        mine = slice(k * rows, (k + 1) * rows)
        out_ref[k] = jnp.concatenate([wo_ref[k], coarse[mine], fine[mine]], axis=0)


def payload_of(left, right, normed, moved, wo):
    chunks, width, lanes = wo.shape
    rows, ch = left.shape[1] * lanes // width, normed.shape[1]
    extra = 2 * (2 * width * ch // lanes // chunks)
    return pl.pallas_call(
        payload_kernel,
        out_shape=jax.ShapeDtypeStruct((chunks, width + extra, lanes), BF),
        scratch_shapes=[pltpu.VMEM((rows, LANES), F32)],
        compiler_params=params(),
        name="payload",
    )(left, right, normed, moved, wo)


def align_kernel(left_ref, right_ref, x_ref, factor_ref, behind_ref, grad_ref, held):
    del behind_ref
    left_rows(left_ref, held)
    right_grad = right_ref[...]
    width, rows = right_grad.shape
    padded = jnp.concatenate([right_grad, jnp.zeros((LANES - width, rows), F32)], axis=0)
    lane = lax.broadcasted_iota(jnp.int32, (rows, LANES), 1)
    both = jnp.where(lane < width, held[...], pltpu.roll(padded.T, width, 1))
    normed, scale = standardize(x_ref)
    deriv = dot(both[:, : 2 * width].astype(BF), factor_ref[...])
    mean = jnp.mean(deriv, axis=-1, keepdims=True)
    along = jnp.mean(deriv * normed, axis=-1, keepdims=True)
    grad_ref[...] = (scale * (deriv - mean - normed * along)).astype(BF).reshape(grad_ref.shape)


def align(left, right, x, factor, behind):
    return pl.pallas_call(
        align_kernel,
        grid=(1,),
        in_specs=[whole(v.shape) for v in (left, right, x, factor, behind)],
        out_specs=whole(x.shape),
        out_shape=jax.ShapeDtypeStruct(x.shape, BF),
        scratch_shapes=[pltpu.VMEM((x.shape[0] * x.shape[1], LANES), F32)],
        compiler_params=params(),
        name="align",
    )(left, right, x, factor, behind)


def total_kernel(in_ref, out_ref):
    out_ref[...] = jnp.sum(in_ref[...].astype(F32), axis=0)


def total(parts):
    return pl.pallas_call(
        total_kernel,
        out_shape=jax.ShapeDtypeStruct(parts.shape[1:], F32),
        compiler_params=params(),
        name="total",
    )(parts)


def hold_kernel(in_ref, behind_ref, out_ref):
    del behind_ref
    out_ref[...] = in_ref[...]


def hold(value, behind):
    return pl.pallas_call(
        hold_kernel,
        grid=(1,),
        in_specs=[whole(value.shape), pl.BlockSpec(memory_space=pl.ANY)],
        out_specs=whole(value.shape),
        out_shape=jax.ShapeDtypeStruct(value.shape, value.dtype),
        compiler_params=params(),
        name="hold",
    )(value, behind)


def refine(parts, width):
    added = jnp.sum(parts, axis=0)
    mid = (added.shape[0] + width) // 2
    return added[:width], added[width:mid] + added[mid:]


def total_copies_kernel(width, in_ref, behind_ref, out_ref):
    del behind_ref
    main, rest = refine(in_ref[...].astype(F32), width)
    coarse = rest.astype(BF)
    fine = (rest - coarse.astype(F32)).astype(BF)
    summed = jnp.concatenate([main.astype(BF), coarse, fine], axis=0)
    for k in range(out_ref.shape[0]):
        out_ref[k] = summed


def total_copies(parts, width, copies, behind):
    return pl.pallas_call(
        functools.partial(total_copies_kernel, width),
        in_specs=[whole(parts.shape), whole(behind.shape)],
        out_specs=whole((copies,) + parts.shape[1:]),
        grid=(1,),
        out_shape=jax.ShapeDtypeStruct((copies,) + parts.shape[1:], BF),
        compiler_params=params(),
        name="total_copies",
    )(parts, behind)


def last_kernel(in_ref, factor_ref, weight_ref):
    chunks, tall, lanes = in_ref.shape
    width = weight_ref.shape[0] // chunks
    mid = (tall + width) // 2
    rest = []
    for d in range(chunks):
        weight_ref[pl.ds(d, width, stride=chunks), :] = in_ref[d, :width, :].astype(F32)
        tail = in_ref[d, width:, :].astype(F32)
        rest.append(tail[: mid - width] + tail[mid - width :])
    stacked = jnp.concatenate(rest, axis=0)
    both, ch = factor_ref.shape
    for k in range(ch // lanes):
        factor_ref[:, k * lanes : (k + 1) * lanes] = stacked[k * both : (k + 1) * both]


def last(parts, width, factor_shape):
    chunks, tall, lanes = parts.shape
    return pl.pallas_call(
        last_kernel,
        out_shape=[
            jax.ShapeDtypeStruct(factor_shape, F32),
            jax.ShapeDtypeStruct((chunks * width, lanes), F32),
        ],
        compiler_params=params(),
        name="last",
    )(parts)


def exchange(parts, axis):
    return lax.all_to_all(parts, axis, 0, 0, tiled=True)


def exchange_in(parts, groups):
    return lax.all_to_all(parts, ("seq", "res"), 0, 0, axis_index_groups=groups, tiled=True)


def grouped(pairs, nr, key):
    found = {}
    for a, b in pairs:
        found.setdefault(key(a, b), []).append(a * nr + b)
    return list(found.values())


def body(nq, nr, homolog_matrix, factor_matrix, output_weight, output_bias, pairwise_cotangent):
    width = factor_matrix.shape[1] // 2
    inv_count = 1.0 / (2 * nq)
    pairs = [(a, b) for a in range(nq) for b in range(nr)]
    line = nq // 2
    outer = grouped(pairs, nr, lambda a, b: (a % line, b % 2))
    inner = grouped(pairs, nr, lambda a, b: (a // line, b // 2))
    there = [(s * nr + r, (r // 2) * nr + 2 * s + r % 2) for s in range(nq) for r in range(nr)]
    back = [(b, a) for a, b in there]
    bias = output_bias.reshape(1, -1)
    factor = factor_matrix.T
    left_mine, packed = before(homolog_matrix, factor)
    moved = lax.ppermute(packed, ("seq", "res"), there)
    left_all = exchange(jnp.broadcast_to(left_mine, (nq,) + left_mine.shape), "seq")
    tail = moved[homolog_matrix.shape[0] * homolog_matrix.shape[1] :]
    right_moved = jnp.concatenate(jnp.split(tail, tail.shape[1] // LANES, axis=1), axis=0)
    grad, w = grad_outer(output_weight, pairwise_cotangent, width)
    right_all = exchange(jnp.broadcast_to(right_moved, (nr,) + right_moved.shape), "res")
    right_in = exchange(right(left_all, grad, width, inv_count), "res")
    rt, left_out = left(right_all, grad, inv_count)
    left_in = exchange(left_out, "seq")
    wo, rows = weight(left_all, rt, pairwise_cotangent, width, inv_count)
    right_total = total(right_in)
    payload = payload_of(left_in, right_total, packed, moved, wo)
    residues = pairwise_cotangent.shape[0]
    steps = residues // 8
    cuts = [0, (steps + 2) // 3, (2 * steps + 2) // 3, steps]
    summed = exchange_in(payload, outer)
    pair, token = pair_part(rows, w, rt, bias, residues, cuts[0], cuts[1], payload)
    payload = total_copies(summed, width, len(inner[0]), token)
    summed = exchange_in(payload, inner)
    pair, token = pair_part(rows, w, rt, bias, residues, cuts[1], cuts[2], payload, pair)
    payload = total_copies(summed, width, len(outer[0]), token)
    summed = exchange_in(payload, outer)
    right_back = lax.ppermute(hold(right_total, payload), ("seq", "res"), back)
    pairwise_update, token = pair_part(rows, w, rt, bias, residues, cuts[2], cuts[3], payload, pair)
    alignment_gradient = align(left_in, right_back, homolog_matrix, factor, token)
    factor_grad, output_weight_gradient = last(summed, width, factor.shape)
    return (pairwise_update, alignment_gradient, factor_grad.T, output_weight_gradient)


def solution(mesh):
    placed = (P("seq", "res", None), P(), P(), P(), P("res", "seq", None))
    return jax.shard_map(
        functools.partial(body, mesh.shape["seq"], mesh.shape["res"]),
        mesh=mesh,
        in_specs=placed,
        out_specs=(P("res", "seq", None), P("seq", "res", None), P(), P()),
        check_vma=False,
    )
```

```python
import functools

import jax
import jax.numpy as jnp
import numpy as np
from jax import lax
from jax.experimental import pallas as pl
from jax.experimental.pallas import tpu as pltpu
from jax.sharding import PartitionSpec as P

BF = jnp.bfloat16
F32 = jnp.float32
LANES = 128
MIB = 1024 * 1024
BIG = 56
NN = (((1,), (0,)), ((), ()))
NT = (((1,), (1,)), ((), ()))


def dot(a, b, dims=NN):
    return lax.dot_general(a, b, dims, preferred_element_type=F32)


def params(size=16):
    return pltpu.CompilerParams(vmem_limit_bytes=size * MIB)


def whole(shape):
    return pl.BlockSpec(shape, lambda *_: (0,) * len(shape))


def low_lanes(shape, width):
    return lax.broadcasted_iota(jnp.int32, shape, len(shape) - 1) < width


def cost(flops):
    return pl.CostEstimate(flops=flops, bytes_accessed=4_000_000, transcendentals=0)


def standardize(x_ref):
    seqs, residues, ch = x_ref.shape
    x = x_ref[...].reshape(seqs * residues, ch).astype(F32)
    centered = x - jnp.mean(x, axis=-1, keepdims=True)
    variance = jnp.mean(centered * centered, axis=-1, keepdims=True)
    scale = lax.rsqrt(variance + 1e-05)
    return centered * scale, scale


def before_kernel(x_ref, factor_ref, left_ref, packed_ref, held):
    normed = standardize(x_ref)[0].astype(BF)
    packed_ref[: normed.shape[0], :] = normed
    mapped = dot(normed, factor_ref[...], NT)
    rows, both = mapped.shape
    width = both // 2
    per = LANES // width
    padded = jnp.concatenate([mapped, jnp.zeros((rows, LANES - both), F32)], axis=1)
    turned = padded.T[width:both].astype(BF)
    parts = normed.shape[1] // LANES
    few = width // parts
    packed_ref[normed.shape[0] :, :] = jnp.concatenate([turned[k * few : (k + 1) * few] for k in range(parts)], axis=1)
    held[...] = padded
    lane = lax.broadcasted_iota(jnp.int32, (rows // per, LANES), 1)
    total = held[pl.ds(0, rows // per, stride=per), :]
    for low in range(1, per):
        part = pltpu.roll(held[pl.ds(low, rows // per, stride=per), :], low * width, 1)
        total = jnp.where(lane < low * width, total, part)
    left_ref[...] = total.astype(BF)


def before(x, factor):
    width = factor.shape[0] // 2
    rows = x.shape[0] * x.shape[1]
    return pl.pallas_call(
        before_kernel,
        out_shape=[
            jax.ShapeDtypeStruct((rows * width // LANES, LANES), BF),
            jax.ShapeDtypeStruct((rows + width * rows // x.shape[2], x.shape[2]), BF),
        ],
        scratch_shapes=[pltpu.VMEM((rows, LANES), F32)],
        compiler_params=params(BIG),
        name="before",
    )(x, factor)


def rows_of(ref, index, count):
    return ref.at[pl.ds(pl.multiple_of(index * count, count), count), :]


def grad_outer_kernel(parts, given_ref, cot_ref, out_ref, w_ref, wide, held, sems):
    residues, cols, ch = cot_ref.shape
    block = residues // parts
    count = out_ref.shape[0] // parts
    width = count // block
    group = LANES // width
    wide[...] = given_ref[...].astype(F32)
    depth = wide.shape[0] // width
    for d in range(depth):
        w_ref[d * width : (d + 1) * width, :] = wide[pl.ds(d, width, stride=depth), :].astype(BF)

    def copy(index):
        return pltpu.make_async_copy(rows_of(held, index, count), rows_of(out_ref, index, count), sems.at[index])

    def one(index, carry):
        for n in range(block // 2):
            cot = cot_ref[pl.ds(index * block + 2 * n, 2)].reshape(2 * cols, ch)
            for m in range(w_ref.shape[0] // LANES):
                piece = dot(w_ref[m * LANES : (m + 1) * LANES, :], cot, NT).astype(BF)
                for k in range(2):
                    row = pl.multiple_of(index * count + (2 * n + k) * width, width)
                    for g in range(group):
                        d = m * group + g
                        held[pl.ds(row, width), d * cols : (d + 1) * cols] = piece[
                            g * width : (g + 1) * width, k * cols : (k + 1) * cols
                        ]
        copy(index).start()
        return carry

    lax.fori_loop(0, parts, one, 0)
    lax.fori_loop(0, parts, lambda index, carry: copy(index).wait(), None)


def grad_outer(w, cot, width, parts=8):
    residues, cols, ch = cot.shape
    shape = (residues * width, w.shape[0] // width * cols)
    return pl.pallas_call(
        functools.partial(grad_outer_kernel, parts),
        in_specs=[whole(w.shape), whole(cot.shape)],
        out_specs=[pl.BlockSpec(memory_space=pl.ANY), whole(w.shape)],
        grid=(1,),
        out_shape=[jax.ShapeDtypeStruct(shape, BF), jax.ShapeDtypeStruct(w.shape, BF)],
        scratch_shapes=[pltpu.VMEM(w.shape, F32), pltpu.VMEM(shape, BF), pltpu.SemaphoreType.DMA((parts,))],
        compiler_params=params(BIG),
        cost_estimate=cost(8_000_000_000),
        name="grad_outer",
    )(w, cot)


def right_kernel(inv_count, parts, mine_ref, slots_ref, recv_ref, grad_ref, out_ref, held, sems, spread, rows, sums, totals):
    nq, tall, lanes = recv_ref.shape
    width = out_ref.shape[1]
    count = grad_ref.shape[0] // parts
    half = lanes // 2

    def copy(index):
        return pltpu.make_async_copy(rows_of(grad_ref, index, count), rows_of(held, index, count), sems.at[index])

    lax.fori_loop(0, parts, lambda index, carry: copy(index).start(), None)
    spread[...] = recv_ref[...].reshape(nq * tall, lanes).astype(F32) * inv_count
    for s in range(2):
        for t in range(tall // 2):
            rows[t * lanes // count, s * nq : (s + 1) * nq, t * lanes % count : t * lanes % count + lanes] = spread[
                pl.ds(s * (tall // 2) + t, nq, stride=tall), :
            ].astype(BF)
    sums[...] = jnp.zeros_like(sums)

    def one(index, carry):
        copy(index).wait()
        sums[...] += dot(rows[index], rows_of(held, index, count)[...])
        return carry

    lax.fori_loop(0, parts, one, 0)
    low = low_lanes((nq, lanes), half)
    for d in range(width):
        a = sums[:nq, d * lanes : (d + 1) * lanes]
        b = sums[nq:, d * lanes : (d + 1) * lanes]
        totals[pl.ds(d, nq, stride=2 * width), :] = jnp.where(low, a, pltpu.roll(b, half, 1))
        totals[pl.ds(width + d, nq, stride=2 * width), :] = jnp.where(low, pltpu.roll(a, half, 1), b)
    for r in range(2 * nq):
        out_ref[r] = totals[pl.ds(pl.multiple_of(slots_ref[mine_ref[0], r] * width, width), width), :].astype(BF)


def right(mine, slots, recv, grad, width, inv_count, parts=8):
    nq, tall, lanes = recv.shape
    depth, wide = grad.shape
    out = (2 * nq, width, lanes)
    return pl.pallas_call(
        functools.partial(right_kernel, inv_count, parts),
        in_specs=[pl.BlockSpec(memory_space=pltpu.SMEM)] * 2 + [whole(recv.shape), pl.BlockSpec(memory_space=pl.ANY)],
        out_specs=whole(out),
        grid=(1,),
        out_shape=jax.ShapeDtypeStruct(out, BF),
        scratch_shapes=[
            pltpu.VMEM(grad.shape, BF),
            pltpu.SemaphoreType.DMA((parts,)),
            pltpu.VMEM((nq * tall, lanes), F32),
            pltpu.VMEM((parts, 2 * nq, depth // parts), BF),
            pltpu.VMEM((2 * nq, wide), F32),
            pltpu.VMEM((2 * nq * width, lanes), F32),
        ],
        compiler_params=params(BIG),
        cost_estimate=cost(8_000_000_000),
        name="right",
    )(mine, slots, recv, grad)


def left_kernel(inv_count, parts, mine_ref, slots_ref, recv_ref, grad_ref, rt_ref, out_ref, held, sems, spread, rows, totals):
    nr, width, lanes = recv_ref.shape
    nq = nr // 2
    tall = out_ref.shape[1]
    count = grad_ref.shape[0] // parts

    def copy(index):
        return pltpu.make_async_copy(rows_of(grad_ref, index, count), rows_of(held, index, count), sems.at[index])

    lax.fori_loop(0, parts, lambda index, carry: copy(index).start(), None)
    for r in range(nr):
        spread[pl.ds(pl.multiple_of(slots_ref[mine_ref[0], r] * width, width), width), :] = recv_ref[r].astype(F32)
    low = low_lanes((nq, lanes), lanes // 2)
    for d in range(width):
        a = spread[pl.ds(d, nq, stride=2 * width), :]
        b = spread[pl.ds(width + d, nq, stride=2 * width), :]
        first = jnp.where(low, a, pltpu.roll(b, lanes // 2, 1)).astype(BF)
        second = jnp.where(low, pltpu.roll(a, lanes // 2, 1), b).astype(BF)
        rt_ref[(2 * d) * nq : (2 * d + 1) * nq, :] = first
        rt_ref[(2 * d + 1) * nq : (2 * d + 2) * nq, :] = second
        rows[:nq, d * lanes : (d + 1) * lanes] = first
        rows[nq:, d * lanes : (d + 1) * lanes] = second

    def one(index, carry):
        copy(index).wait()
        part = dot(rows[...], rows_of(held, index, count)[...], NT) * inv_count
        for k in range(count // lanes):
            for s in range(2):
                t = s * (tall // 2) + index * (count // lanes) + k
                totals[pl.ds(t, nq, stride=tall), :] = part[s * nq : (s + 1) * nq, k * lanes : (k + 1) * lanes]
        return carry

    lax.fori_loop(0, parts, one, 0)
    out_ref[...] = totals[...].reshape(out_ref.shape).astype(BF)


def left(mine, slots, recv, grad, inv_count, parts=8):
    nr, width, lanes = recv.shape
    nq = nr // 2
    deep, wide = grad.shape
    out = (nq, 2 * deep // lanes, lanes)
    return pl.pallas_call(
        functools.partial(left_kernel, inv_count, parts),
        in_specs=[pl.BlockSpec(memory_space=pltpu.SMEM)] * 2 + [whole(recv.shape), pl.BlockSpec(memory_space=pl.ANY)],
        out_specs=[whole((nr * width, lanes)), whole(out)],
        grid=(1,),
        out_shape=[jax.ShapeDtypeStruct((nr * width, lanes), BF), jax.ShapeDtypeStruct(out, BF)],
        scratch_shapes=[
            pltpu.VMEM(grad.shape, BF),
            pltpu.SemaphoreType.DMA((parts,)),
            pltpu.VMEM((nr * width, lanes), F32),
            pltpu.VMEM((nr, wide), BF),
            pltpu.VMEM((out[0] * out[1], lanes), F32),
        ],
        compiler_params=params(BIG),
        cost_estimate=cost(8_000_000_000),
        name="left",
    )(mine, slots, recv, grad)


def weight_kernel(inv_count, recv_ref, rt_ref, cot_ref, out_ref, rows_ref, spread, held, totals):
    step = pl.program_id(0)
    nq, tall, lanes = recv_ref.shape
    block, cols, ch = cot_ref.shape
    depth, width, _ = out_ref.shape
    seqs = 2 * nq
    group = lanes // seqs

    @pl.when(step == 0)
    def _():
        per = lanes // width
        spread[...] = recv_ref[...].reshape(nq * tall, lanes).astype(F32) * inv_count
        for t in range(tall // 2):
            for s in range(2):
                part = spread[pl.ds(s * (tall // 2) + t, nq, stride=tall), :]
                for low in range(per):
                    mine = part if low == 0 else pltpu.roll(part, lanes - low * width, 1)
                    row = ((t * per + low) * 2 + s) * nq
                    rows_ref[row : row + nq, :] = mine.astype(BF)

    cot = jnp.concatenate([cot_ref[i] for i in range(block)], axis=1)
    for m in range(depth // group):
        mine = rt_ref[m * lanes : (m + 1) * lanes, :]
        for n in range(block // 2):
            piece = dot(mine, cot[:, n * 2 * ch : (n + 1) * 2 * ch]).astype(BF)
            for g in range(group):
                d = m * group + g
                for k in range(2):
                    i = 2 * n + k
                    held[i * seqs : (i + 1) * seqs, d * ch : (d + 1) * ch] = piece[
                        g * seqs : (g + 1) * seqs, k * ch : (k + 1) * ch
                    ]
    count = block * seqs
    start = pl.multiple_of(step * count, count)
    turned = jnp.concatenate(
        [
            rows_ref[pl.ds(start + k * lanes, lanes), :].astype(F32).T[:width].astype(BF)
            for k in range(count // lanes)
        ],
        axis=1,
    )
    part = dot(turned, held[...])

    @pl.when(step == 0)
    def _():
        totals[...] = part

    @pl.when(step > 0)
    def _():
        totals[...] += part

    @pl.when(step == pl.num_programs(0) - 1)
    def _():
        for d in range(depth):
            out_ref[d] = totals[:, d * ch : (d + 1) * ch].astype(BF)


def weight(recv, rt, cot, width, inv_count, block=8):
    nq, tall, lanes = recv.shape
    residues, cols, ch = cot.shape
    seqs = 2 * nq
    depth = rt.shape[0] // seqs
    out = (depth, width, ch)
    return pl.pallas_call(
        functools.partial(weight_kernel, inv_count),
        grid=(residues // block,),
        in_specs=[whole(recv.shape), whole(rt.shape), pl.BlockSpec((block, cols, ch), lambda s: (s, 0, 0))],
        out_specs=[whole(out), whole((residues * seqs, lanes))],
        out_shape=[jax.ShapeDtypeStruct(out, BF), jax.ShapeDtypeStruct((residues * seqs, lanes), BF)],
        scratch_shapes=[
            pltpu.VMEM((nq * tall, lanes), F32),
            pltpu.VMEM((block * seqs, depth * ch), BF),
            pltpu.VMEM((width, depth * ch), F32),
        ],
        compiler_params=params(BIG),
        cost_estimate=cost(16_000_000_000),
        name="weight",
    )(recv, rt, cot)


def pair_kernel(rows_ref, w_ref, rt_ref, bias_ref, *refs):
    out_ref, token_ref, r, held = refs[-4:]
    block, cols, ch = out_ref.shape
    depth = held.shape[0]
    seqs = rows_ref.shape[0] // block
    width = w_ref.shape[0] * seqs // depth

    @pl.when(pl.program_id(0) == 0)
    def _():
        token_ref[...] = jnp.zeros_like(token_ref)
        for k in range(depth // LANES):
            r[:, k * LANES : (k + 1) * LANES] = rt_ref[k * LANES : (k + 1) * LANES, :].astype(F32).T.astype(BF)

    rows = rows_ref[:, :width]
    for n in range(depth // seqs // 2):
        w = jnp.concatenate([w_ref[(2 * n + k) * width : (2 * n + k + 1) * width, :] for k in range(2)], axis=1)
        piece = dot(rows, w).astype(BF)
        for k in range(2):
            d = 2 * n + k
            for i in range(block):
                held[d * seqs : (d + 1) * seqs, i * ch : (i + 1) * ch] = piece[
                    i * seqs : (i + 1) * seqs, k * ch : (k + 1) * ch
                ]
    bias = bias_ref[...]
    mine = r[...]
    for n in range(block // 2):
        piece = dot(mine, held[:, n * 2 * ch : (n + 1) * 2 * ch])
        for k in range(2):
            out_ref[2 * n + k] = (piece[:, k * ch : (k + 1) * ch] + bias).astype(BF)


def pair_part(rows, w, rt, bias, residues, begin, end, behind, held=None, block=8):
    count, lanes = rows.shape
    seqs = count // residues
    depth, cols = rt.shape
    ch = bias.shape[1]
    anywhere = pl.BlockSpec(memory_space=pl.ANY)
    more = [behind] + ([] if held is None else [held])
    return pl.pallas_call(
        pair_kernel,
        grid=(end - begin,),
        in_specs=[
            pl.BlockSpec((block * seqs, lanes), lambda s: (s + begin, 0)),
            whole(w.shape),
            whole(rt.shape),
            whole(bias.shape),
        ]
        + [anywhere] * len(more),
        out_specs=[pl.BlockSpec((block, cols, ch), lambda s: (s + begin, 0, 0)), whole((8, LANES))],
        out_shape=[
            jax.ShapeDtypeStruct((residues, cols, ch), BF),
            jax.ShapeDtypeStruct((8, LANES), F32),
        ],
        scratch_shapes=[pltpu.VMEM((cols, depth), BF), pltpu.VMEM((depth, block * ch), BF)],
        input_output_aliases={} if held is None else {5: 0},
        compiler_params=params(BIG),
        cost_estimate=cost(6_000_000_000),
        name="pair_part",
    )(rows, w, rt, bias, *more)


def left_rows(left_ref, held):
    added = jnp.sum(left_ref[...].astype(F32), axis=0)
    per = held.shape[0] // added.shape[0]
    width = LANES // per
    for low in range(per):
        part = added if low == 0 else pltpu.roll(added, LANES - low * width, 1)
        held[pl.ds(low, added.shape[0], stride=per), :] = part


def payload_kernel(left_ref, right_ref, normed_ref, moved_ref, wo_ref, out_ref, held):
    left_rows(left_ref, held)
    chunks, width, _ = wo_ref.shape
    left_grad = held[...].T[:width].astype(BF)
    factor_part = jnp.concatenate(
        [dot(left_grad, normed_ref[: held.shape[0], :]), dot(right_ref[...].astype(BF), moved_ref[: held.shape[0], :])], axis=0
    )
    stacked = jnp.concatenate(
        [factor_part[:, k * LANES : (k + 1) * LANES] for k in range(factor_part.shape[1] // LANES)], axis=0
    )
    coarse = stacked.astype(BF)
    fine = (stacked - coarse.astype(F32)).astype(BF)
    rows = stacked.shape[0] // chunks
    for k in range(chunks):
        mine = slice(k * rows, (k + 1) * rows)
        out_ref[k] = jnp.concatenate([wo_ref[k], coarse[mine], fine[mine]], axis=0)


def payload_of(left, right, normed, moved, wo):
    chunks, width, lanes = wo.shape
    rows, ch = left.shape[1] * lanes // width, normed.shape[1]
    extra = 2 * (2 * width * ch // lanes // chunks)
    return pl.pallas_call(
        payload_kernel,
        out_shape=jax.ShapeDtypeStruct((chunks, width + extra, lanes), BF),
        scratch_shapes=[pltpu.VMEM((rows, LANES), F32)],
        compiler_params=params(),
        name="payload",
    )(left, right, normed, moved, wo)


def align_kernel(left_ref, right_ref, x_ref, factor_ref, behind_ref, grad_ref, held):
    del behind_ref
    left_rows(left_ref, held)
    right_grad = right_ref[...]
    width, rows = right_grad.shape
    padded = jnp.concatenate([right_grad, jnp.zeros((LANES - width, rows), F32)], axis=0)
    lane = lax.broadcasted_iota(jnp.int32, (rows, LANES), 1)
    both = jnp.where(lane < width, held[...], pltpu.roll(padded.T, width, 1))
    normed, scale = standardize(x_ref)
    deriv = dot(both[:, : 2 * width].astype(BF), factor_ref[...])
    mean = jnp.mean(deriv, axis=-1, keepdims=True)
    along = jnp.mean(deriv * normed, axis=-1, keepdims=True)
    grad_ref[...] = (scale * (deriv - mean - normed * along)).astype(BF).reshape(grad_ref.shape)


def align(left, right, x, factor, behind):
    return pl.pallas_call(
        align_kernel,
        grid=(1,),
        in_specs=[whole(v.shape) for v in (left, right, x, factor)] + [pl.BlockSpec(memory_space=pl.ANY)],
        out_specs=whole(x.shape),
        out_shape=jax.ShapeDtypeStruct(x.shape, BF),
        scratch_shapes=[pltpu.VMEM((x.shape[0] * x.shape[1], LANES), F32)],
        compiler_params=params(),
        name="align",
    )(left, right, x, factor, behind)


def total_kernel(in_ref, out_ref):
    out_ref[...] = jnp.sum(in_ref[...].astype(F32), axis=0)


def total(parts):
    return pl.pallas_call(
        total_kernel,
        out_shape=jax.ShapeDtypeStruct(parts.shape[1:], F32),
        compiler_params=params(),
        name="total",
    )(parts)


def hold_kernel(in_ref, behind_ref, out_ref):
    del behind_ref
    out_ref[...] = in_ref[...]


def hold(value, behind):
    return pl.pallas_call(
        hold_kernel,
        grid=(1,),
        in_specs=[whole(value.shape), pl.BlockSpec(memory_space=pl.ANY)],
        out_specs=whole(value.shape),
        out_shape=jax.ShapeDtypeStruct(value.shape, value.dtype),
        compiler_params=params(),
        name="hold",
    )(value, behind)


def refine(parts, width):
    added = jnp.sum(parts, axis=0)
    mid = (added.shape[0] + width) // 2
    return added[:width], added[width:mid] + added[mid:]


def total_copies_kernel(width, in_ref, behind_ref, out_ref):
    del behind_ref
    main, rest = refine(in_ref[...].astype(F32), width)
    coarse = rest.astype(BF)
    fine = (rest - coarse.astype(F32)).astype(BF)
    summed = jnp.concatenate([main.astype(BF), coarse, fine], axis=0)
    for k in range(out_ref.shape[0]):
        out_ref[k] = summed


def total_copies(parts, width, copies, behind):
    return pl.pallas_call(
        functools.partial(total_copies_kernel, width),
        in_specs=[whole(parts.shape), whole(behind.shape)],
        out_specs=whole((copies,) + parts.shape[1:]),
        grid=(1,),
        out_shape=jax.ShapeDtypeStruct((copies,) + parts.shape[1:], BF),
        compiler_params=params(),
        name="total_copies",
    )(parts, behind)


def last_kernel(in_ref, factor_ref, weight_ref):
    chunks, tall, lanes = in_ref.shape
    width = weight_ref.shape[0] // chunks
    mid = (tall + width) // 2
    rest = []
    for d in range(chunks):
        weight_ref[pl.ds(d, width, stride=chunks), :] = in_ref[d, :width, :].astype(F32)
        tail = in_ref[d, width:, :].astype(F32)
        rest.append(tail[: mid - width] + tail[mid - width :])
    stacked = jnp.concatenate(rest, axis=0)
    both, ch = factor_ref.shape
    for k in range(ch // lanes):
        factor_ref[:, k * lanes : (k + 1) * lanes] = stacked[k * both : (k + 1) * both]


def last(parts, width, factor_shape):
    chunks, tall, lanes = parts.shape
    return pl.pallas_call(
        last_kernel,
        out_shape=[
            jax.ShapeDtypeStruct(factor_shape, F32),
            jax.ShapeDtypeStruct((chunks * width, lanes), F32),
        ],
        compiler_params=params(),
        name="last",
    )(parts)


def exchange(parts, axis):
    return lax.all_to_all(parts, axis, 0, 0, tiled=True)


def exchange_in(parts, groups):
    return lax.all_to_all(parts, ("seq", "res"), 0, 0, axis_index_groups=groups, tiled=True)


def grouped(pairs, nr, key):
    found = {}
    for a, b in pairs:
        found.setdefault(key(a, b), []).append(a * nr + b)
    return list(found.values())


def ring(a, b, size):
    return min((a - b) % size, (b - a) % size)


def nearest(nq, side):
    line = nq // 2
    found = []
    for q in range(nq):
        x, y = q // side, q % side

        def hops(s, t):
            along_y = ring(s // line * side + y, q // line * side + t % side, 2 * side)
            return ring(s % line, q % line, line) + along_y + ring(x, t // side, side)

        for most in range(4 * nq):
            held = {}

            def place(s, seen):
                for t in sorted(range(nq), key=lambda t: hops(s, t)):
                    if hops(s, t) <= most and t not in seen:
                        seen.add(t)
                        if t not in held or place(held[t], seen):
                            held[t] = s
                            return True
                return False

            if all(place(s, set()) for s in range(nq)):
                break
        found.append([held[t] for t in range(nq)])
    return found


def body(nq, nr, homolog_matrix, factor_matrix, output_weight, output_bias, pairwise_cotangent):
    width = factor_matrix.shape[1] // 2
    inv_count = 1.0 / (2 * nq)
    pairs = [(a, b) for a in range(nq) for b in range(nr)]
    line = nq // 2
    outer = grouped(pairs, nr, lambda a, b: (a % line, b % 2))
    inner = grouped(pairs, nr, lambda a, b: (a // line, b // 2))
    senders = nearest(nq, 4)
    halves = [(q, t, h) for q in range(nq) for t in range(nq) for h in range(2)]
    there = [(senders[q][t] * nr + 2 * q + h, q * nr + 2 * t + h) for q, t, h in halves]
    table = np.array([2 * senders[q][t] + h for q, t, h in halves], np.int32).reshape(nq, nr)
    slots = jnp.asarray(table)
    mine = lax.axis_index("seq").astype(jnp.int32).reshape(1)
    back = [(b, a) for a, b in there]
    bias = output_bias.reshape(1, -1)
    factor = factor_matrix.T
    left_mine, packed = before(homolog_matrix, factor)
    moved = lax.ppermute(packed, ("seq", "res"), there)
    left_all = exchange(jnp.broadcast_to(left_mine, (nq,) + left_mine.shape), "seq")
    tail = moved[homolog_matrix.shape[0] * homolog_matrix.shape[1] :]
    right_moved = jnp.concatenate(jnp.split(tail, tail.shape[1] // LANES, axis=1), axis=0)
    grad, w = grad_outer(output_weight, pairwise_cotangent, width)
    right_all = exchange(jnp.broadcast_to(right_moved, (nr,) + right_moved.shape), "res")
    right_in = exchange(right(mine, slots, left_all, grad, width, inv_count), "res")
    rt, left_out = left(mine, slots, right_all, grad, inv_count)
    left_in = exchange(left_out, "seq")
    wo, rows = weight(left_all, rt, pairwise_cotangent, width, inv_count)
    right_total = total(right_in)
    payload = payload_of(left_in, right_total, packed, moved, wo)
    residues = pairwise_cotangent.shape[0]
    steps = residues // 8
    cut = steps // 2
    summed = exchange_in(payload, outer)
    right_back = lax.ppermute(hold(right_total, payload), ("seq", "res"), back)
    payload = total_copies(summed, width, len(inner[0]), right_back)
    summed = exchange_in(payload, inner)
    pair, token = pair_part(rows, w, rt, bias, residues, 0, cut, payload)
    payload = total_copies(summed, width, len(outer[0]), token)
    summed = exchange_in(payload, outer)
    pairwise_update, _ = pair_part(rows, w, rt, bias, residues, cut, steps, payload, pair)
    alignment_gradient = align(left_in, right_back, homolog_matrix, factor, payload)
    factor_grad, output_weight_gradient = last(summed, width, factor.shape)
    return (pairwise_update, alignment_gradient, factor_grad.T, output_weight_gradient)


def solution(mesh):
    placed = (P("seq", "res", None), P(), P(), P(), P("res", "seq", None))
    return jax.shard_map(
        functools.partial(body, mesh.shape["seq"], mesh.shape["res"]),
        mesh=mesh,
        in_specs=placed,
        out_specs=(P("res", "seq", None), P("seq", "res", None), P(), P()),
        check_vma=False,
    )
```

```python
import functools

import jax
import jax.numpy as jnp
import numpy as np
from jax import lax
from jax.experimental import pallas as pl
from jax.experimental.pallas import tpu as pltpu
from jax.sharding import PartitionSpec as P

BF = jnp.bfloat16
F32 = jnp.float32
LANES = 128
MIB = 1024 * 1024
BIG = 56
NN = (((1,), (0,)), ((), ()))
NT = (((1,), (1,)), ((), ()))


def dot(a, b, dims=NN):
    return lax.dot_general(a, b, dims, preferred_element_type=F32)


def params(size=16):
    return pltpu.CompilerParams(vmem_limit_bytes=size * MIB)


def whole(shape):
    return pl.BlockSpec(shape, lambda *_: (0,) * len(shape))


def low_lanes(shape, width):
    return lax.broadcasted_iota(jnp.int32, shape, len(shape) - 1) < width


def cost(flops):
    return pl.CostEstimate(flops=flops, bytes_accessed=4_000_000, transcendentals=0)


def standardize(x_ref):
    seqs, residues, ch = x_ref.shape
    x = x_ref[...].reshape(seqs * residues, ch).astype(F32)
    centered = x - jnp.mean(x, axis=-1, keepdims=True)
    variance = jnp.mean(centered * centered, axis=-1, keepdims=True)
    scale = lax.rsqrt(variance + 1e-05)
    return centered * scale, scale


def before_kernel(x_ref, factor_ref, left_ref, packed_ref, held):
    normed = standardize(x_ref)[0].astype(BF)
    packed_ref[: normed.shape[0], :] = normed
    mapped = dot(normed, factor_ref[...], NT)
    rows, both = mapped.shape
    width = both // 2
    per = LANES // width
    padded = jnp.concatenate([mapped, jnp.zeros((rows, LANES - both), F32)], axis=1)
    turned = padded.T[width:both].astype(BF)
    parts = normed.shape[1] // LANES
    few = width // parts
    packed_ref[normed.shape[0] :, :] = jnp.concatenate([turned[k * few : (k + 1) * few] for k in range(parts)], axis=1)
    held[...] = padded
    lane = lax.broadcasted_iota(jnp.int32, (rows // per, LANES), 1)
    total = held[pl.ds(0, rows // per, stride=per), :]
    for low in range(1, per):
        part = pltpu.roll(held[pl.ds(low, rows // per, stride=per), :], low * width, 1)
        total = jnp.where(lane < low * width, total, part)
    left_ref[...] = total.astype(BF)


def before(x, factor):
    width = factor.shape[0] // 2
    rows = x.shape[0] * x.shape[1]
    return pl.pallas_call(
        before_kernel,
        out_shape=[
            jax.ShapeDtypeStruct((rows * width // LANES, LANES), BF),
            jax.ShapeDtypeStruct((rows + width * rows // x.shape[2], x.shape[2]), BF),
        ],
        scratch_shapes=[pltpu.VMEM((rows, LANES), F32)],
        compiler_params=params(BIG),
        name="before",
    )(x, factor)


def rows_of(ref, index, count):
    return ref.at[pl.ds(pl.multiple_of(index * count, count), count), :]


def grad_outer_kernel(parts, given_ref, cot_ref, out_ref, w_ref, wide, held, sems):
    residues, cols, ch = cot_ref.shape
    block = residues // parts
    count = out_ref.shape[0] // parts
    width = count // block
    group = LANES // width
    wide[...] = given_ref[...].astype(F32)
    depth = wide.shape[0] // width
    for d in range(depth):
        w_ref[d * width : (d + 1) * width, :] = wide[pl.ds(d, width, stride=depth), :].astype(BF)

    def copy(index):
        return pltpu.make_async_copy(rows_of(held, index, count), rows_of(out_ref, index, count), sems.at[index])

    def one(index, carry):
        for n in range(block // 2):
            cot = cot_ref[pl.ds(index * block + 2 * n, 2)].reshape(2 * cols, ch)
            for m in range(w_ref.shape[0] // LANES):
                piece = dot(w_ref[m * LANES : (m + 1) * LANES, :], cot, NT).astype(BF)
                for k in range(2):
                    row = pl.multiple_of(index * count + (2 * n + k) * width, width)
                    for g in range(group):
                        d = m * group + g
                        held[pl.ds(row, width), d * cols : (d + 1) * cols] = piece[
                            g * width : (g + 1) * width, k * cols : (k + 1) * cols
                        ]
        copy(index).start()
        return carry

    lax.fori_loop(0, parts, one, 0)
    lax.fori_loop(0, parts, lambda index, carry: copy(index).wait(), None)


def grad_outer(w, cot, width, parts=8):
    residues, cols, ch = cot.shape
    shape = (residues * width, w.shape[0] // width * cols)
    return pl.pallas_call(
        functools.partial(grad_outer_kernel, parts),
        in_specs=[whole(w.shape), whole(cot.shape)],
        out_specs=[pl.BlockSpec(memory_space=pl.ANY), whole(w.shape)],
        grid=(1,),
        out_shape=[jax.ShapeDtypeStruct(shape, BF), jax.ShapeDtypeStruct(w.shape, BF)],
        scratch_shapes=[pltpu.VMEM(w.shape, F32), pltpu.VMEM(shape, BF), pltpu.SemaphoreType.DMA((parts,))],
        compiler_params=params(BIG),
        cost_estimate=cost(8_000_000_000),
        name="grad_outer",
    )(w, cot)


def right_kernel(inv_count, parts, mine_ref, slots_ref, recv_ref, grad_ref, out_ref, held, sems, spread, rows, sums, totals):
    nq, tall, lanes = recv_ref.shape
    width = out_ref.shape[1]
    count = grad_ref.shape[0] // parts
    half = lanes // 2

    def copy(index):
        return pltpu.make_async_copy(rows_of(grad_ref, index, count), rows_of(held, index, count), sems.at[index])

    lax.fori_loop(0, parts, lambda index, carry: copy(index).start(), None)
    spread[...] = recv_ref[...].reshape(nq * tall, lanes).astype(F32) * inv_count
    for s in range(2):
        for t in range(tall // 2):
            rows[t * lanes // count, s * nq : (s + 1) * nq, t * lanes % count : t * lanes % count + lanes] = spread[
                pl.ds(s * (tall // 2) + t, nq, stride=tall), :
            ].astype(BF)
    sums[...] = jnp.zeros_like(sums)

    def one(index, carry):
        copy(index).wait()
        sums[...] += dot(rows[index], rows_of(held, index, count)[...])
        return carry

    lax.fori_loop(0, parts, one, 0)
    low = low_lanes((nq, lanes), half)
    for d in range(width):
        a = sums[:nq, d * lanes : (d + 1) * lanes]
        b = sums[nq:, d * lanes : (d + 1) * lanes]
        totals[pl.ds(d, nq, stride=2 * width), :] = jnp.where(low, a, pltpu.roll(b, half, 1))
        totals[pl.ds(width + d, nq, stride=2 * width), :] = jnp.where(low, pltpu.roll(a, half, 1), b)
    for r in range(2 * nq):
        out_ref[r] = totals[pl.ds(pl.multiple_of(slots_ref[mine_ref[0], r] * width, width), width), :].astype(BF)


def right(mine, slots, recv, grad, width, inv_count, parts=8):
    nq, tall, lanes = recv.shape
    depth, wide = grad.shape
    out = (2 * nq, width, lanes)
    return pl.pallas_call(
        functools.partial(right_kernel, inv_count, parts),
        in_specs=[pl.BlockSpec(memory_space=pltpu.SMEM)] * 2 + [whole(recv.shape), pl.BlockSpec(memory_space=pl.ANY)],
        out_specs=whole(out),
        grid=(1,),
        out_shape=jax.ShapeDtypeStruct(out, BF),
        scratch_shapes=[
            pltpu.VMEM(grad.shape, BF),
            pltpu.SemaphoreType.DMA((parts,)),
            pltpu.VMEM((nq * tall, lanes), F32),
            pltpu.VMEM((parts, 2 * nq, depth // parts), BF),
            pltpu.VMEM((2 * nq, wide), F32),
            pltpu.VMEM((2 * nq * width, lanes), F32),
        ],
        compiler_params=params(BIG),
        cost_estimate=cost(8_000_000_000),
        name="right",
    )(mine, slots, recv, grad)


def left_kernel(inv_count, parts, mine_ref, slots_ref, recv_ref, grad_ref, rt_ref, out_ref, held, sems, spread, rows, totals):
    nr, width, lanes = recv_ref.shape
    nq = nr // 2
    tall = out_ref.shape[1]
    count = grad_ref.shape[0] // parts

    def copy(index):
        return pltpu.make_async_copy(rows_of(grad_ref, index, count), rows_of(held, index, count), sems.at[index])

    lax.fori_loop(0, parts, lambda index, carry: copy(index).start(), None)
    for r in range(nr):
        spread[pl.ds(pl.multiple_of(slots_ref[mine_ref[0], r] * width, width), width), :] = recv_ref[r].astype(F32)
    low = low_lanes((nq, lanes), lanes // 2)
    for d in range(width):
        a = spread[pl.ds(d, nq, stride=2 * width), :]
        b = spread[pl.ds(width + d, nq, stride=2 * width), :]
        first = jnp.where(low, a, pltpu.roll(b, lanes // 2, 1)).astype(BF)
        second = jnp.where(low, pltpu.roll(a, lanes // 2, 1), b).astype(BF)
        rt_ref[(2 * d) * nq : (2 * d + 1) * nq, :] = first
        rt_ref[(2 * d + 1) * nq : (2 * d + 2) * nq, :] = second
        rows[:nq, d * lanes : (d + 1) * lanes] = first
        rows[nq:, d * lanes : (d + 1) * lanes] = second

    def one(index, carry):
        copy(index).wait()
        part = dot(rows[...], rows_of(held, index, count)[...], NT) * inv_count
        for k in range(count // lanes):
            for s in range(2):
                t = s * (tall // 2) + index * (count // lanes) + k
                totals[pl.ds(t, nq, stride=tall), :] = part[s * nq : (s + 1) * nq, k * lanes : (k + 1) * lanes]
        return carry

    lax.fori_loop(0, parts, one, 0)
    out_ref[...] = totals[...].reshape(out_ref.shape).astype(BF)


def left(mine, slots, recv, grad, inv_count, parts=8):
    nr, width, lanes = recv.shape
    nq = nr // 2
    deep, wide = grad.shape
    out = (nq, 2 * deep // lanes, lanes)
    return pl.pallas_call(
        functools.partial(left_kernel, inv_count, parts),
        in_specs=[pl.BlockSpec(memory_space=pltpu.SMEM)] * 2 + [whole(recv.shape), pl.BlockSpec(memory_space=pl.ANY)],
        out_specs=[whole((nr * width, lanes)), whole(out)],
        grid=(1,),
        out_shape=[jax.ShapeDtypeStruct((nr * width, lanes), BF), jax.ShapeDtypeStruct(out, BF)],
        scratch_shapes=[
            pltpu.VMEM(grad.shape, BF),
            pltpu.SemaphoreType.DMA((parts,)),
            pltpu.VMEM((nr * width, lanes), F32),
            pltpu.VMEM((nr, wide), BF),
            pltpu.VMEM((out[0] * out[1], lanes), F32),
        ],
        compiler_params=params(BIG),
        cost_estimate=cost(8_000_000_000),
        name="left",
    )(mine, slots, recv, grad)


def weight_kernel(inv_count, recv_ref, rt_ref, cot_ref, out_ref, rows_ref, spread, held, totals):
    step = pl.program_id(0)
    nq, tall, lanes = recv_ref.shape
    block, cols, ch = cot_ref.shape
    depth, width, _ = out_ref.shape
    seqs = 2 * nq
    group = lanes // seqs

    @pl.when(step == 0)
    def _():
        per = lanes // width
        spread[...] = recv_ref[...].reshape(nq * tall, lanes).astype(F32) * inv_count
        for t in range(tall // 2):
            for s in range(2):
                part = spread[pl.ds(s * (tall // 2) + t, nq, stride=tall), :]
                for low in range(per):
                    mine = part if low == 0 else pltpu.roll(part, lanes - low * width, 1)
                    row = ((t * per + low) * 2 + s) * nq
                    rows_ref[row : row + nq, :] = mine.astype(BF)

    cot = jnp.concatenate([cot_ref[i] for i in range(block)], axis=1)
    for m in range(depth // group):
        mine = rt_ref[m * lanes : (m + 1) * lanes, :]
        for n in range(block // 2):
            piece = dot(mine, cot[:, n * 2 * ch : (n + 1) * 2 * ch]).astype(BF)
            for g in range(group):
                d = m * group + g
                for k in range(2):
                    i = 2 * n + k
                    held[i * seqs : (i + 1) * seqs, d * ch : (d + 1) * ch] = piece[
                        g * seqs : (g + 1) * seqs, k * ch : (k + 1) * ch
                    ]
    count = block * seqs
    start = pl.multiple_of(step * count, count)
    turned = jnp.concatenate(
        [
            rows_ref[pl.ds(start + k * lanes, lanes), :].astype(F32).T[:width].astype(BF)
            for k in range(count // lanes)
        ],
        axis=1,
    )
    part = dot(turned, held[...])

    @pl.when(step == 0)
    def _():
        totals[...] = part

    @pl.when(step > 0)
    def _():
        totals[...] += part

    @pl.when(step == pl.num_programs(0) - 1)
    def _():
        for d in range(depth):
            out_ref[d] = totals[:, d * ch : (d + 1) * ch].astype(BF)


def weight(recv, rt, cot, width, inv_count, block=8):
    nq, tall, lanes = recv.shape
    residues, cols, ch = cot.shape
    seqs = 2 * nq
    depth = rt.shape[0] // seqs
    out = (depth, width, ch)
    return pl.pallas_call(
        functools.partial(weight_kernel, inv_count),
        grid=(residues // block,),
        in_specs=[whole(recv.shape), whole(rt.shape), pl.BlockSpec((block, cols, ch), lambda s: (s, 0, 0))],
        out_specs=[whole(out), whole((residues * seqs, lanes))],
        out_shape=[jax.ShapeDtypeStruct(out, BF), jax.ShapeDtypeStruct((residues * seqs, lanes), BF)],
        scratch_shapes=[
            pltpu.VMEM((nq * tall, lanes), F32),
            pltpu.VMEM((block * seqs, depth * ch), BF),
            pltpu.VMEM((width, depth * ch), F32),
        ],
        compiler_params=params(BIG),
        cost_estimate=cost(16_000_000_000),
        name="weight",
    )(recv, rt, cot)


def pair_kernel(rows_ref, w_ref, rt_ref, bias_ref, *refs):
    out_ref, token_ref, r, held = refs[-4:]
    block, cols, ch = out_ref.shape
    depth = held.shape[0]
    seqs = rows_ref.shape[0] // block
    width = w_ref.shape[0] * seqs // depth

    @pl.when(pl.program_id(0) == 0)
    def _():
        token_ref[...] = jnp.zeros_like(token_ref)
        for k in range(depth // LANES):
            r[:, k * LANES : (k + 1) * LANES] = rt_ref[k * LANES : (k + 1) * LANES, :].astype(F32).T.astype(BF)

    rows = rows_ref[:, :width]
    for n in range(depth // seqs // 2):
        w = jnp.concatenate([w_ref[(2 * n + k) * width : (2 * n + k + 1) * width, :] for k in range(2)], axis=1)
        piece = dot(rows, w).astype(BF)
        for k in range(2):
            d = 2 * n + k
            for i in range(block):
                held[d * seqs : (d + 1) * seqs, i * ch : (i + 1) * ch] = piece[
                    i * seqs : (i + 1) * seqs, k * ch : (k + 1) * ch
                ]
    bias = bias_ref[...]
    mine = r[...]
    for n in range(block // 2):
        piece = dot(mine, held[:, n * 2 * ch : (n + 1) * 2 * ch])
        for k in range(2):
            out_ref[2 * n + k] = (piece[:, k * ch : (k + 1) * ch] + bias).astype(BF)


def pair_part(rows, w, rt, bias, residues, begin, end, behind, held=None, block=8):
    count, lanes = rows.shape
    seqs = count // residues
    depth, cols = rt.shape
    ch = bias.shape[1]
    anywhere = pl.BlockSpec(memory_space=pl.ANY)
    more = [behind] + ([] if held is None else [held])
    return pl.pallas_call(
        pair_kernel,
        grid=(end - begin,),
        in_specs=[
            pl.BlockSpec((block * seqs, lanes), lambda s: (s + begin, 0)),
            whole(w.shape),
            whole(rt.shape),
            whole(bias.shape),
        ]
        + [anywhere] * len(more),
        out_specs=[pl.BlockSpec((block, cols, ch), lambda s: (s + begin, 0, 0)), whole((8, LANES))],
        out_shape=[
            jax.ShapeDtypeStruct((residues, cols, ch), BF),
            jax.ShapeDtypeStruct((8, LANES), F32),
        ],
        scratch_shapes=[pltpu.VMEM((cols, depth), BF), pltpu.VMEM((depth, block * ch), BF)],
        input_output_aliases={} if held is None else {5: 0},
        compiler_params=params(40),
        cost_estimate=cost(6_000_000_000),
        name="pair_part",
    )(rows, w, rt, bias, *more)


def left_rows(left_ref, held):
    added = jnp.sum(left_ref[...].astype(F32), axis=0)
    per = held.shape[0] // added.shape[0]
    width = LANES // per
    for low in range(per):
        part = added if low == 0 else pltpu.roll(added, LANES - low * width, 1)
        held[pl.ds(low, added.shape[0], stride=per), :] = part


def payload_kernel(left_ref, right_ref, normed_ref, moved_ref, wo_ref, out_ref, held):
    left_rows(left_ref, held)
    chunks, width, _ = wo_ref.shape
    left_grad = held[...].T[:width].astype(BF)
    factor_part = jnp.concatenate(
        [dot(left_grad, normed_ref[: held.shape[0], :]), dot(right_ref[...].astype(BF), moved_ref[: held.shape[0], :])], axis=0
    )
    stacked = jnp.concatenate(
        [factor_part[:, k * LANES : (k + 1) * LANES] for k in range(factor_part.shape[1] // LANES)], axis=0
    )
    coarse = stacked.astype(BF)
    fine = (stacked - coarse.astype(F32)).astype(BF)
    rows = stacked.shape[0] // chunks
    for k in range(chunks):
        mine = slice(k * rows, (k + 1) * rows)
        out_ref[k] = jnp.concatenate([wo_ref[k], coarse[mine], fine[mine]], axis=0)


def payload_of(left, right, normed, moved, wo):
    chunks, width, lanes = wo.shape
    rows, ch = left.shape[1] * lanes // width, normed.shape[1]
    extra = 2 * (2 * width * ch // lanes // chunks)
    return pl.pallas_call(
        payload_kernel,
        out_shape=jax.ShapeDtypeStruct((chunks, width + extra, lanes), BF),
        scratch_shapes=[pltpu.VMEM((rows, LANES), F32)],
        compiler_params=params(),
        name="payload",
    )(left, right, normed, moved, wo)


def align_kernel(left_ref, right_ref, x_ref, factor_ref, behind_ref, grad_ref, held):
    del behind_ref
    left_rows(left_ref, held)
    right_grad = right_ref[...]
    width, rows = right_grad.shape
    padded = jnp.concatenate([right_grad, jnp.zeros((LANES - width, rows), F32)], axis=0)
    lane = lax.broadcasted_iota(jnp.int32, (rows, LANES), 1)
    both = jnp.where(lane < width, held[...], pltpu.roll(padded.T, width, 1))
    normed, scale = standardize(x_ref)
    deriv = dot(both[:, : 2 * width].astype(BF), factor_ref[...])
    mean = jnp.mean(deriv, axis=-1, keepdims=True)
    along = jnp.mean(deriv * normed, axis=-1, keepdims=True)
    grad_ref[...] = (scale * (deriv - mean - normed * along)).astype(BF).reshape(grad_ref.shape)


def align(left, right, x, factor, behind):
    return pl.pallas_call(
        align_kernel,
        grid=(1,),
        in_specs=[whole(v.shape) for v in (left, right, x, factor)] + [pl.BlockSpec(memory_space=pl.ANY)],
        out_specs=whole(x.shape),
        out_shape=jax.ShapeDtypeStruct(x.shape, BF),
        scratch_shapes=[pltpu.VMEM((x.shape[0] * x.shape[1], LANES), F32)],
        compiler_params=params(),
        name="align",
    )(left, right, x, factor, behind)


def total_kernel(in_ref, out_ref):
    out_ref[...] = jnp.sum(in_ref[...].astype(F32), axis=0)


def total(parts):
    return pl.pallas_call(
        total_kernel,
        out_shape=jax.ShapeDtypeStruct(parts.shape[1:], F32),
        compiler_params=params(),
        name="total",
    )(parts)


def hold_kernel(in_ref, behind_ref, out_ref):
    del behind_ref
    out_ref[...] = in_ref[...]


def hold(value, behind):
    return pl.pallas_call(
        hold_kernel,
        grid=(1,),
        in_specs=[whole(value.shape), pl.BlockSpec(memory_space=pl.ANY)],
        out_specs=whole(value.shape),
        out_shape=jax.ShapeDtypeStruct(value.shape, value.dtype),
        compiler_params=params(),
        name="hold",
    )(value, behind)


def refine(parts, width):
    added = jnp.sum(parts, axis=0)
    mid = (added.shape[0] + width) // 2
    return added[:width], added[width:mid] + added[mid:]


def total_copies_kernel(width, in_ref, behind_ref, out_ref):
    del behind_ref
    main, rest = refine(in_ref[...].astype(F32), width)
    coarse = rest.astype(BF)
    fine = (rest - coarse.astype(F32)).astype(BF)
    summed = jnp.concatenate([main.astype(BF), coarse, fine], axis=0)
    for k in range(out_ref.shape[0]):
        out_ref[k] = summed


def total_copies(parts, width, copies, behind):
    return pl.pallas_call(
        functools.partial(total_copies_kernel, width),
        in_specs=[whole(parts.shape), whole(behind.shape)],
        out_specs=whole((copies,) + parts.shape[1:]),
        grid=(1,),
        out_shape=jax.ShapeDtypeStruct((copies,) + parts.shape[1:], BF),
        compiler_params=params(),
        name="total_copies",
    )(parts, behind)


def last_kernel(in_ref, factor_ref, weight_ref):
    chunks, tall, lanes = in_ref.shape
    width = weight_ref.shape[0] // chunks
    mid = (tall + width) // 2
    rest = []
    for d in range(chunks):
        weight_ref[pl.ds(d, width, stride=chunks), :] = in_ref[d, :width, :].astype(F32)
        tail = in_ref[d, width:, :].astype(F32)
        rest.append(tail[: mid - width] + tail[mid - width :])
    stacked = jnp.concatenate(rest, axis=0)
    both, ch = factor_ref.shape
    for k in range(ch // lanes):
        factor_ref[:, k * lanes : (k + 1) * lanes] = stacked[k * both : (k + 1) * both]


def last(parts, width, factor_shape):
    chunks, tall, lanes = parts.shape
    return pl.pallas_call(
        last_kernel,
        out_shape=[
            jax.ShapeDtypeStruct(factor_shape, F32),
            jax.ShapeDtypeStruct((chunks * width, lanes), F32),
        ],
        compiler_params=params(),
        name="last",
    )(parts)


def exchange(parts, axis):
    return lax.all_to_all(parts, axis, 0, 0, tiled=True)


def exchange_in(parts, groups):
    return lax.all_to_all(parts, ("seq", "res"), 0, 0, axis_index_groups=groups, tiled=True)


def grouped(pairs, nr, key):
    found = {}
    for a, b in pairs:
        found.setdefault(key(a, b), []).append(a * nr + b)
    return list(found.values())


def ring(a, b, size):
    return min((a - b) % size, (b - a) % size)


def nearest(nq, side):
    line = nq // 2
    found = []
    for q in range(nq):
        x, y = q // side, q % side

        def hops(s, t):
            along_y = ring(s // line * side + y, q // line * side + t % side, 2 * side)
            return ring(s % line, q % line, line) + along_y + ring(x, t // side, side)

        for most in range(4 * nq):
            held = {}

            def place(s, seen):
                for t in sorted(range(nq), key=lambda t: hops(s, t)):
                    if hops(s, t) <= most and t not in seen:
                        seen.add(t)
                        if t not in held or place(held[t], seen):
                            held[t] = s
                            return True
                return False

            if all(place(s, set()) for s in range(nq)):
                break
        found.append([held[t] for t in range(nq)])
    return found


def body(nq, nr, homolog_matrix, factor_matrix, output_weight, output_bias, pairwise_cotangent):
    width = factor_matrix.shape[1] // 2
    inv_count = 1.0 / (2 * nq)
    pairs = [(a, b) for a in range(nq) for b in range(nr)]
    line = nq // 2
    outer = grouped(pairs, nr, lambda a, b: (a % line, b % 2))
    inner = grouped(pairs, nr, lambda a, b: (a // line, b // 2))
    senders = nearest(nq, 4)
    halves = [(q, t, h) for q in range(nq) for t in range(nq) for h in range(2)]
    there = [(senders[q][t] * nr + 2 * q + h, q * nr + 2 * t + h) for q, t, h in halves]
    table = np.array([2 * senders[q][t] + h for q, t, h in halves], np.int32).reshape(nq, nr)
    slots = jnp.asarray(table)
    mine = lax.axis_index("seq").astype(jnp.int32).reshape(1)
    back = [(b, a) for a, b in there]
    bias = output_bias.reshape(1, -1)
    factor = factor_matrix.T
    left_mine, packed = before(homolog_matrix, factor)
    moved = lax.ppermute(packed, ("seq", "res"), there)
    left_all = exchange(jnp.broadcast_to(left_mine, (nq,) + left_mine.shape), "seq")
    tail = moved[homolog_matrix.shape[0] * homolog_matrix.shape[1] :]
    right_moved = jnp.concatenate(jnp.split(tail, tail.shape[1] // LANES, axis=1), axis=0)
    grad, w = grad_outer(output_weight, pairwise_cotangent, width)
    right_all = exchange(jnp.broadcast_to(right_moved, (nr,) + right_moved.shape), "res")
    right_in = exchange(right(mine, slots, left_all, grad, width, inv_count), "res")
    rt, left_out = left(mine, slots, right_all, grad, inv_count)
    left_in = exchange(left_out, "seq")
    wo, rows = weight(left_all, rt, pairwise_cotangent, width, inv_count)
    right_total = total(right_in)
    payload = payload_of(left_in, right_total, packed, moved, wo)
    residues = pairwise_cotangent.shape[0]
    steps = residues // 8
    cut = steps // 2
    summed = exchange_in(payload, outer)
    right_back = lax.ppermute(hold(right_total, payload), ("seq", "res"), back)
    payload = total_copies(summed, width, len(inner[0]), right_back)
    summed = exchange_in(payload, inner)
    pair, token = pair_part(rows, w, rt, bias, residues, 0, cut, payload)
    payload = total_copies(summed, width, len(outer[0]), token)
    summed = exchange_in(payload, outer)
    pairwise_update, _ = pair_part(rows, w, rt, bias, residues, cut, steps, payload, pair)
    alignment_gradient = align(left_in, right_back, homolog_matrix, factor, payload)
    factor_grad, output_weight_gradient = last(summed, width, factor.shape)
    return (pairwise_update, alignment_gradient, factor_grad.T, output_weight_gradient)


def solution(mesh):
    placed = (P("seq", "res", None), P(), P(), P(), P("res", "seq", None))
    return jax.shard_map(
        functools.partial(body, mesh.shape["seq"], mesh.shape["res"]),
        mesh=mesh,
        in_specs=placed,
        out_specs=(P("res", "seq", None), P("seq", "res", None), P(), P()),
        check_vma=False,
    )
```

```python
import functools

import jax
import jax.numpy as jnp
import numpy as np
from jax import lax
from jax.experimental import pallas as pl
from jax.experimental.pallas import tpu as pltpu
from jax.sharding import PartitionSpec as P

BF = jnp.bfloat16
F32 = jnp.float32
LANES = 128
MIB = 1024 * 1024
BIG = 56
NN = (((1,), (0,)), ((), ()))
NT = (((1,), (1,)), ((), ()))


def dot(a, b, dims=NN):
    return lax.dot_general(a, b, dims, preferred_element_type=F32)


def params(size=16):
    return pltpu.CompilerParams(vmem_limit_bytes=size * MIB)


def whole(shape):
    return pl.BlockSpec(shape, lambda *_: (0,) * len(shape))


def low_lanes(shape, width):
    return lax.broadcasted_iota(jnp.int32, shape, len(shape) - 1) < width


def cost(flops):
    return pl.CostEstimate(flops=flops, bytes_accessed=4_000_000, transcendentals=0)


def standardize(x_ref):
    seqs, residues, ch = x_ref.shape
    x = x_ref[...].reshape(seqs * residues, ch).astype(F32)
    centered = x - jnp.mean(x, axis=-1, keepdims=True)
    variance = jnp.mean(centered * centered, axis=-1, keepdims=True)
    scale = lax.rsqrt(variance + 1e-05)
    return centered * scale, scale


def before_kernel(x_ref, factor_ref, left_ref, packed_ref, held):
    normed = standardize(x_ref)[0].astype(BF)
    packed_ref[: normed.shape[0], :] = normed
    mapped = dot(normed, factor_ref[...], NT)
    rows, both = mapped.shape
    width = both // 2
    per = LANES // width
    padded = jnp.concatenate([mapped, jnp.zeros((rows, LANES - both), F32)], axis=1)
    turned = padded.T[width:both].astype(BF)
    parts = normed.shape[1] // LANES
    few = width // parts
    packed_ref[normed.shape[0] :, :] = jnp.concatenate([turned[k * few : (k + 1) * few] for k in range(parts)], axis=1)
    held[...] = padded
    lane = lax.broadcasted_iota(jnp.int32, (rows // per, LANES), 1)
    total = held[pl.ds(0, rows // per, stride=per), :]
    for low in range(1, per):
        part = pltpu.roll(held[pl.ds(low, rows // per, stride=per), :], low * width, 1)
        total = jnp.where(lane < low * width, total, part)
    left_ref[...] = total.astype(BF)


def before(x, factor):
    width = factor.shape[0] // 2
    rows = x.shape[0] * x.shape[1]
    return pl.pallas_call(
        before_kernel,
        out_shape=[
            jax.ShapeDtypeStruct((rows * width // LANES, LANES), BF),
            jax.ShapeDtypeStruct((rows + width * rows // x.shape[2], x.shape[2]), BF),
        ],
        scratch_shapes=[pltpu.VMEM((rows, LANES), F32)],
        compiler_params=params(BIG),
        name="before",
    )(x, factor)


def rows_of(ref, index, count):
    return ref.at[pl.ds(pl.multiple_of(index * count, count), count), :]


def grad_outer_kernel(parts, given_ref, cot_ref, out_ref, w_ref, wide, held, sems):
    residues, cols, ch = cot_ref.shape
    block = residues // parts
    count = out_ref.shape[0] // parts
    width = count // block
    group = LANES // width
    wide[...] = given_ref[...].astype(F32)
    depth = wide.shape[0] // width
    for d in range(depth):
        w_ref[d * width : (d + 1) * width, :] = wide[pl.ds(d, width, stride=depth), :].astype(BF)

    def copy(index):
        return pltpu.make_async_copy(rows_of(held, index, count), rows_of(out_ref, index, count), sems.at[index])

    def one(index, carry):
        for n in range(block // 2):
            cot = cot_ref[pl.ds(index * block + 2 * n, 2)].reshape(2 * cols, ch)
            for m in range(w_ref.shape[0] // LANES):
                piece = dot(w_ref[m * LANES : (m + 1) * LANES, :], cot, NT).astype(BF)
                for k in range(2):
                    row = pl.multiple_of(index * count + (2 * n + k) * width, width)
                    for g in range(group):
                        d = m * group + g
                        held[pl.ds(row, width), d * cols : (d + 1) * cols] = piece[
                            g * width : (g + 1) * width, k * cols : (k + 1) * cols
                        ]
        copy(index).start()
        return carry

    lax.fori_loop(0, parts, one, 0)
    lax.fori_loop(0, parts, lambda index, carry: copy(index).wait(), None)


def grad_outer(w, cot, width, parts=8):
    residues, cols, ch = cot.shape
    shape = (residues * width, w.shape[0] // width * cols)
    return pl.pallas_call(
        functools.partial(grad_outer_kernel, parts),
        in_specs=[whole(w.shape), whole(cot.shape)],
        out_specs=[pl.BlockSpec(memory_space=pl.ANY), whole(w.shape)],
        grid=(1,),
        out_shape=[jax.ShapeDtypeStruct(shape, BF), jax.ShapeDtypeStruct(w.shape, BF)],
        scratch_shapes=[pltpu.VMEM(w.shape, F32), pltpu.VMEM(shape, BF), pltpu.SemaphoreType.DMA((parts,))],
        compiler_params=params(BIG),
        cost_estimate=cost(8_000_000_000),
        name="grad_outer",
    )(w, cot)


def right_kernel(inv_count, parts, mine_ref, slots_ref, recv_ref, grad_ref, out_ref, held, sems, spread, rows, sums, totals):
    nq, tall, lanes = recv_ref.shape
    width = out_ref.shape[1]
    count = grad_ref.shape[0] // parts
    half = lanes // 2

    def copy(index):
        return pltpu.make_async_copy(rows_of(grad_ref, index, count), rows_of(held, index, count), sems.at[index])

    lax.fori_loop(0, parts, lambda index, carry: copy(index).start(), None)
    spread[...] = recv_ref[...].reshape(nq * tall, lanes).astype(F32) * inv_count
    for s in range(2):
        for t in range(tall // 2):
            rows[t * lanes // count, s * nq : (s + 1) * nq, t * lanes % count : t * lanes % count + lanes] = spread[
                pl.ds(s * (tall // 2) + t, nq, stride=tall), :
            ].astype(BF)
    sums[...] = jnp.zeros_like(sums)

    def one(index, carry):
        copy(index).wait()
        sums[...] += dot(rows[index], rows_of(held, index, count)[...])
        return carry

    lax.fori_loop(0, parts, one, 0)
    low = low_lanes((nq, lanes), half)
    for d in range(width):
        a = sums[:nq, d * lanes : (d + 1) * lanes]
        b = sums[nq:, d * lanes : (d + 1) * lanes]
        totals[pl.ds(d, nq, stride=2 * width), :] = jnp.where(low, a, pltpu.roll(b, half, 1))
        totals[pl.ds(width + d, nq, stride=2 * width), :] = jnp.where(low, pltpu.roll(a, half, 1), b)
    for r in range(2 * nq):
        out_ref[r] = totals[pl.ds(pl.multiple_of(slots_ref[mine_ref[0], r] * width, width), width), :].astype(BF)


def right(mine, slots, recv, grad, width, inv_count, parts=8):
    nq, tall, lanes = recv.shape
    depth, wide = grad.shape
    out = (2 * nq, width, lanes)
    return pl.pallas_call(
        functools.partial(right_kernel, inv_count, parts),
        in_specs=[pl.BlockSpec(memory_space=pltpu.SMEM)] * 2 + [whole(recv.shape), pl.BlockSpec(memory_space=pl.ANY)],
        out_specs=whole(out),
        grid=(1,),
        out_shape=jax.ShapeDtypeStruct(out, BF),
        scratch_shapes=[
            pltpu.VMEM(grad.shape, BF),
            pltpu.SemaphoreType.DMA((parts,)),
            pltpu.VMEM((nq * tall, lanes), F32),
            pltpu.VMEM((parts, 2 * nq, depth // parts), BF),
            pltpu.VMEM((2 * nq, wide), F32),
            pltpu.VMEM((2 * nq * width, lanes), F32),
        ],
        compiler_params=params(BIG),
        cost_estimate=cost(8_000_000_000),
        name="right",
    )(mine, slots, recv, grad)


def left_kernel(inv_count, parts, mine_ref, slots_ref, recv_ref, grad_ref, rt_ref, out_ref, held, sems, spread, rows, totals):
    nr, width, lanes = recv_ref.shape
    nq = nr // 2
    tall = out_ref.shape[1]
    count = grad_ref.shape[0] // parts

    def copy(index):
        return pltpu.make_async_copy(rows_of(grad_ref, index, count), rows_of(held, index, count), sems.at[index])

    lax.fori_loop(0, parts, lambda index, carry: copy(index).start(), None)
    for r in range(nr):
        spread[pl.ds(pl.multiple_of(slots_ref[mine_ref[0], r] * width, width), width), :] = recv_ref[r].astype(F32)
    low = low_lanes((nq, lanes), lanes // 2)
    for d in range(width):
        a = spread[pl.ds(d, nq, stride=2 * width), :]
        b = spread[pl.ds(width + d, nq, stride=2 * width), :]
        first = jnp.where(low, a, pltpu.roll(b, lanes // 2, 1)).astype(BF)
        second = jnp.where(low, pltpu.roll(a, lanes // 2, 1), b).astype(BF)
        rt_ref[(2 * d) * nq : (2 * d + 1) * nq, :] = first
        rt_ref[(2 * d + 1) * nq : (2 * d + 2) * nq, :] = second
        rows[:nq, d * lanes : (d + 1) * lanes] = first
        rows[nq:, d * lanes : (d + 1) * lanes] = second

    def one(index, carry):
        copy(index).wait()
        part = dot(rows[...], rows_of(held, index, count)[...], NT) * inv_count
        for k in range(count // lanes):
            for s in range(2):
                t = s * (tall // 2) + index * (count // lanes) + k
                totals[pl.ds(t, nq, stride=tall), :] = part[s * nq : (s + 1) * nq, k * lanes : (k + 1) * lanes]
        return carry

    lax.fori_loop(0, parts, one, 0)
    out_ref[...] = totals[...].reshape(out_ref.shape).astype(BF)


def left(mine, slots, recv, grad, inv_count, parts=8):
    nr, width, lanes = recv.shape
    nq = nr // 2
    deep, wide = grad.shape
    out = (nq, 2 * deep // lanes, lanes)
    return pl.pallas_call(
        functools.partial(left_kernel, inv_count, parts),
        in_specs=[pl.BlockSpec(memory_space=pltpu.SMEM)] * 2 + [whole(recv.shape), pl.BlockSpec(memory_space=pl.ANY)],
        out_specs=[whole((nr * width, lanes)), whole(out)],
        grid=(1,),
        out_shape=[jax.ShapeDtypeStruct((nr * width, lanes), BF), jax.ShapeDtypeStruct(out, BF)],
        scratch_shapes=[
            pltpu.VMEM(grad.shape, BF),
            pltpu.SemaphoreType.DMA((parts,)),
            pltpu.VMEM((nr * width, lanes), F32),
            pltpu.VMEM((nr, wide), BF),
            pltpu.VMEM((out[0] * out[1], lanes), F32),
        ],
        compiler_params=params(BIG),
        cost_estimate=cost(8_000_000_000),
        name="left",
    )(mine, slots, recv, grad)


def weight_kernel(inv_count, recv_ref, rt_ref, cot_ref, out_ref, rows_ref, spread, held, totals):
    step = pl.program_id(0)
    nq, tall, lanes = recv_ref.shape
    block, cols, ch = cot_ref.shape
    depth, width, _ = out_ref.shape
    seqs = 2 * nq
    group = lanes // seqs

    @pl.when(step == 0)
    def _():
        per = lanes // width
        spread[...] = recv_ref[...].reshape(nq * tall, lanes).astype(F32) * inv_count
        for t in range(tall // 2):
            for s in range(2):
                part = spread[pl.ds(s * (tall // 2) + t, nq, stride=tall), :]
                for low in range(per):
                    mine = part if low == 0 else pltpu.roll(part, lanes - low * width, 1)
                    row = ((t * per + low) * 2 + s) * nq
                    rows_ref[row : row + nq, :] = mine.astype(BF)

    cot = jnp.concatenate([cot_ref[i] for i in range(block)], axis=1)
    for m in range(depth // group):
        mine = rt_ref[m * lanes : (m + 1) * lanes, :]
        for n in range(block // 2):
            piece = dot(mine, cot[:, n * 2 * ch : (n + 1) * 2 * ch]).astype(BF)
            for g in range(group):
                d = m * group + g
                for k in range(2):
                    i = 2 * n + k
                    held[i * seqs : (i + 1) * seqs, d * ch : (d + 1) * ch] = piece[
                        g * seqs : (g + 1) * seqs, k * ch : (k + 1) * ch
                    ]
    count = block * seqs
    start = pl.multiple_of(step * count, count)
    turned = jnp.concatenate(
        [
            rows_ref[pl.ds(start + k * lanes, lanes), :].astype(F32).T[:width].astype(BF)
            for k in range(count // lanes)
        ],
        axis=1,
    )
    part = dot(turned, held[...])

    @pl.when(step == 0)
    def _():
        totals[...] = part

    @pl.when(step > 0)
    def _():
        totals[...] += part

    @pl.when(step == pl.num_programs(0) - 1)
    def _():
        for d in range(depth):
            out_ref[d] = totals[:, d * ch : (d + 1) * ch].astype(BF)


def weight(recv, rt, cot, width, inv_count, block=8):
    nq, tall, lanes = recv.shape
    residues, cols, ch = cot.shape
    seqs = 2 * nq
    depth = rt.shape[0] // seqs
    out = (depth, width, ch)
    return pl.pallas_call(
        functools.partial(weight_kernel, inv_count),
        grid=(residues // block,),
        in_specs=[whole(recv.shape), whole(rt.shape), pl.BlockSpec((block, cols, ch), lambda s: (s, 0, 0))],
        out_specs=[whole(out), whole((residues * seqs, lanes))],
        out_shape=[jax.ShapeDtypeStruct(out, BF), jax.ShapeDtypeStruct((residues * seqs, lanes), BF)],
        scratch_shapes=[
            pltpu.VMEM((nq * tall, lanes), F32),
            pltpu.VMEM((block * seqs, depth * ch), BF),
            pltpu.VMEM((width, depth * ch), F32),
        ],
        compiler_params=params(BIG),
        cost_estimate=cost(16_000_000_000),
        name="weight",
    )(recv, rt, cot)


def pair_kernel(rows_ref, w_ref, rt_ref, bias_ref, *refs):
    out_ref, token_ref, r, held = refs[-4:]
    block, cols, ch = out_ref.shape
    depth = held.shape[0]
    seqs = rows_ref.shape[0] // block
    width = w_ref.shape[0] * seqs // depth

    @pl.when(pl.program_id(0) == 0)
    def _():
        token_ref[...] = jnp.zeros_like(token_ref)
        for k in range(depth // LANES):
            r[:, k * LANES : (k + 1) * LANES] = rt_ref[k * LANES : (k + 1) * LANES, :].astype(F32).T.astype(BF)

    rows = rows_ref[:, :width]
    for n in range(depth // seqs // 2):
        w = jnp.concatenate([w_ref[(2 * n + k) * width : (2 * n + k + 1) * width, :] for k in range(2)], axis=1)
        piece = dot(rows, w).astype(BF)
        for k in range(2):
            d = 2 * n + k
            for i in range(block):
                held[d * seqs : (d + 1) * seqs, i * ch : (i + 1) * ch] = piece[
                    i * seqs : (i + 1) * seqs, k * ch : (k + 1) * ch
                ]
    bias = bias_ref[...]
    mine = r[...]
    for n in range(block // 2):
        piece = dot(mine, held[:, n * 2 * ch : (n + 1) * 2 * ch])
        for k in range(2):
            out_ref[2 * n + k] = (piece[:, k * ch : (k + 1) * ch] + bias).astype(BF)


def pair_part(rows, w, rt, bias, residues, begin, end, behind, held=None, block=8):
    count, lanes = rows.shape
    seqs = count // residues
    depth, cols = rt.shape
    ch = bias.shape[1]
    anywhere = pl.BlockSpec(memory_space=pl.ANY)
    more = [behind] + ([] if held is None else [held])
    return pl.pallas_call(
        pair_kernel,
        grid=(end - begin,),
        in_specs=[
            pl.BlockSpec((block * seqs, lanes), lambda s: (s + begin, 0)),
            whole(w.shape),
            whole(rt.shape),
            whole(bias.shape),
        ]
        + [anywhere] * len(more),
        out_specs=[pl.BlockSpec((block, cols, ch), lambda s: (s + begin, 0, 0)), whole((8, LANES))],
        out_shape=[
            jax.ShapeDtypeStruct((residues, cols, ch), BF),
            jax.ShapeDtypeStruct((8, LANES), F32),
        ],
        scratch_shapes=[pltpu.VMEM((cols, depth), BF), pltpu.VMEM((depth, block * ch), BF)],
        input_output_aliases={} if held is None else {5: 0},
        compiler_params=params(40),
        cost_estimate=cost(6_000_000_000),
        name="pair_part",
    )(rows, w, rt, bias, *more)


def left_rows(left_ref, held):
    added = jnp.sum(left_ref[...].astype(F32), axis=0)
    per = held.shape[0] // added.shape[0]
    width = LANES // per
    for low in range(per):
        part = added if low == 0 else pltpu.roll(added, LANES - low * width, 1)
        held[pl.ds(low, added.shape[0], stride=per), :] = part


def payload_kernel(left_ref, right_ref, normed_ref, moved_ref, wo_ref, out_ref, held):
    left_rows(left_ref, held)
    chunks, width, _ = wo_ref.shape
    left_grad = held[...].T[:width].astype(BF)
    factor_part = jnp.concatenate(
        [dot(left_grad, normed_ref[: held.shape[0], :]), dot(right_ref[...].astype(BF), moved_ref[: held.shape[0], :])], axis=0
    )
    stacked = jnp.concatenate(
        [factor_part[:, k * LANES : (k + 1) * LANES] for k in range(factor_part.shape[1] // LANES)], axis=0
    )
    coarse = stacked.astype(BF)
    fine = (stacked - coarse.astype(F32)).astype(BF)
    rows = stacked.shape[0] // chunks
    for k in range(chunks):
        mine = slice(k * rows, (k + 1) * rows)
        out_ref[k] = jnp.concatenate([wo_ref[k], coarse[mine], fine[mine]], axis=0)


def payload_of(left, right, normed, moved, wo):
    chunks, width, lanes = wo.shape
    rows, ch = left.shape[1] * lanes // width, normed.shape[1]
    extra = 2 * (2 * width * ch // lanes // chunks)
    return pl.pallas_call(
        payload_kernel,
        out_shape=jax.ShapeDtypeStruct((chunks, width + extra, lanes), BF),
        scratch_shapes=[pltpu.VMEM((rows, LANES), F32)],
        compiler_params=params(BIG),
        name="payload",
    )(left, right, normed, moved, wo)


def align_kernel(left_ref, right_ref, x_ref, factor_ref, behind_ref, grad_ref, held):
    del behind_ref
    left_rows(left_ref, held)
    right_grad = right_ref[...]
    width, rows = right_grad.shape
    padded = jnp.concatenate([right_grad, jnp.zeros((LANES - width, rows), F32)], axis=0)
    lane = lax.broadcasted_iota(jnp.int32, (rows, LANES), 1)
    both = jnp.where(lane < width, held[...], pltpu.roll(padded.T, width, 1))
    normed, scale = standardize(x_ref)
    deriv = dot(both[:, : 2 * width].astype(BF), factor_ref[...])
    mean = jnp.mean(deriv, axis=-1, keepdims=True)
    along = jnp.mean(deriv * normed, axis=-1, keepdims=True)
    grad_ref[...] = (scale * (deriv - mean - normed * along)).astype(BF).reshape(grad_ref.shape)


def align(left, right, x, factor, behind):
    return pl.pallas_call(
        align_kernel,
        grid=(1,),
        in_specs=[whole(v.shape) for v in (left, right, x, factor)] + [pl.BlockSpec(memory_space=pl.ANY)],
        out_specs=whole(x.shape),
        out_shape=jax.ShapeDtypeStruct(x.shape, BF),
        scratch_shapes=[pltpu.VMEM((x.shape[0] * x.shape[1], LANES), F32)],
        compiler_params=params(),
        name="align",
    )(left, right, x, factor, behind)


def total_kernel(in_ref, out_ref):
    out_ref[...] = jnp.sum(in_ref[...].astype(F32), axis=0)


def total(parts):
    return pl.pallas_call(
        total_kernel,
        out_shape=jax.ShapeDtypeStruct(parts.shape[1:], F32),
        compiler_params=params(),
        name="total",
    )(parts)


def hold_kernel(in_ref, behind_ref, out_ref):
    del behind_ref
    out_ref[...] = in_ref[...]


def hold(value, behind):
    return pl.pallas_call(
        hold_kernel,
        grid=(1,),
        in_specs=[whole(value.shape), pl.BlockSpec(memory_space=pl.ANY)],
        out_specs=whole(value.shape),
        out_shape=jax.ShapeDtypeStruct(value.shape, value.dtype),
        compiler_params=params(),
        name="hold",
    )(value, behind)


def refine(parts, width):
    added = jnp.sum(parts, axis=0)
    mid = (added.shape[0] + width) // 2
    return added[:width], added[width:mid] + added[mid:]


def total_copies_kernel(width, in_ref, behind_ref, out_ref):
    del behind_ref
    main, rest = refine(in_ref[...].astype(F32), width)
    coarse = rest.astype(BF)
    fine = (rest - coarse.astype(F32)).astype(BF)
    summed = jnp.concatenate([main.astype(BF), coarse, fine], axis=0)
    for k in range(out_ref.shape[0]):
        out_ref[k] = summed


def total_copies(parts, width, copies, behind):
    return pl.pallas_call(
        functools.partial(total_copies_kernel, width),
        in_specs=[whole(parts.shape), whole(behind.shape)],
        out_specs=whole((copies,) + parts.shape[1:]),
        grid=(1,),
        out_shape=jax.ShapeDtypeStruct((copies,) + parts.shape[1:], BF),
        compiler_params=params(),
        name="total_copies",
    )(parts, behind)


def last_kernel(in_ref, factor_ref, weight_ref):
    chunks, tall, lanes = in_ref.shape
    width = weight_ref.shape[0] // chunks
    mid = (tall + width) // 2
    rest = []
    for d in range(chunks):
        weight_ref[pl.ds(d, width, stride=chunks), :] = in_ref[d, :width, :].astype(F32)
        tail = in_ref[d, width:, :].astype(F32)
        rest.append(tail[: mid - width] + tail[mid - width :])
    stacked = jnp.concatenate(rest, axis=0)
    both, ch = factor_ref.shape
    for k in range(ch // lanes):
        factor_ref[:, k * lanes : (k + 1) * lanes] = stacked[k * both : (k + 1) * both]


def last(parts, width, factor_shape):
    chunks, tall, lanes = parts.shape
    return pl.pallas_call(
        last_kernel,
        out_shape=[
            jax.ShapeDtypeStruct(factor_shape, F32),
            jax.ShapeDtypeStruct((chunks * width, lanes), F32),
        ],
        compiler_params=params(),
        name="last",
    )(parts)


def exchange(parts, axis):
    return lax.all_to_all(parts, axis, 0, 0, tiled=True)


def exchange_in(parts, groups):
    return lax.all_to_all(parts, ("seq", "res"), 0, 0, axis_index_groups=groups, tiled=True)


def grouped(pairs, nr, key):
    found = {}
    for a, b in pairs:
        found.setdefault(key(a, b), []).append(a * nr + b)
    return list(found.values())


def ring(a, b, size):
    return min((a - b) % size, (b - a) % size)


def nearest(nq, side):
    line = nq // 2
    found = []
    for q in range(nq):
        x, y = q // side, q % side

        def hops(s, t):
            along_y = ring(s // line * side + y, q // line * side + t % side, 2 * side)
            return ring(s % line, q % line, line) + along_y + ring(x, t // side, side)

        for most in range(4 * nq):
            held = {}

            def place(s, seen):
                for t in sorted(range(nq), key=lambda t: hops(s, t)):
                    if hops(s, t) <= most and t not in seen:
                        seen.add(t)
                        if t not in held or place(held[t], seen):
                            held[t] = s
                            return True
                return False

            if all(place(s, set()) for s in range(nq)):
                break
        found.append([held[t] for t in range(nq)])
    return found


def body(nq, nr, homolog_matrix, factor_matrix, output_weight, output_bias, pairwise_cotangent):
    width = factor_matrix.shape[1] // 2
    inv_count = 1.0 / (2 * nq)
    pairs = [(a, b) for a in range(nq) for b in range(nr)]
    line = nq // 2
    outer = grouped(pairs, nr, lambda a, b: (a % line, b % 2))
    inner = grouped(pairs, nr, lambda a, b: (a // line, b // 2))
    senders = nearest(nq, 4)
    halves = [(q, t, h) for q in range(nq) for t in range(nq) for h in range(2)]
    there = [(senders[q][t] * nr + 2 * q + h, q * nr + 2 * t + h) for q, t, h in halves]
    table = np.array([2 * senders[q][t] + h for q, t, h in halves], np.int32).reshape(nq, nr)
    slots = jnp.asarray(table)
    mine = lax.axis_index("seq").astype(jnp.int32).reshape(1)
    back = [(b, a) for a, b in there]
    bias = output_bias.reshape(1, -1)
    factor = factor_matrix.T
    left_mine, packed = before(homolog_matrix, factor)
    moved = lax.ppermute(packed, ("seq", "res"), there)
    left_all = exchange(jnp.broadcast_to(left_mine, (nq,) + left_mine.shape), "seq")
    tail = moved[homolog_matrix.shape[0] * homolog_matrix.shape[1] :]
    right_moved = jnp.concatenate(jnp.split(tail, tail.shape[1] // LANES, axis=1), axis=0)
    grad, w = grad_outer(output_weight, pairwise_cotangent, width)
    right_all = exchange(jnp.broadcast_to(right_moved, (nr,) + right_moved.shape), "res")
    right_in = exchange(right(mine, slots, left_all, grad, width, inv_count), "res")
    rt, left_out = left(mine, slots, right_all, grad, inv_count)
    left_in = exchange(left_out, "seq")
    wo, rows = weight(left_all, rt, pairwise_cotangent, width, inv_count)
    right_total = total(right_in)
    payload = payload_of(left_in, right_total, packed, moved, wo)
    residues = pairwise_cotangent.shape[0]
    steps = residues // 8
    cut = steps // 2
    summed = exchange_in(payload, outer)
    right_back = lax.ppermute(hold(right_total, payload), ("seq", "res"), back)
    payload = total_copies(summed, width, len(inner[0]), right_back)
    summed = exchange_in(payload, inner)
    pair, token = pair_part(rows, w, rt, bias, residues, 0, cut, payload)
    payload = total_copies(summed, width, len(outer[0]), token)
    summed = exchange_in(payload, outer)
    pairwise_update, _ = pair_part(rows, w, rt, bias, residues, cut, steps, payload, pair)
    alignment_gradient = align(left_in, right_back, homolog_matrix, factor, payload)
    factor_grad, output_weight_gradient = last(summed, width, factor.shape)
    return (pairwise_update, alignment_gradient, factor_grad.T, output_weight_gradient)


def solution(mesh):
    placed = (P("seq", "res", None), P(), P(), P(), P("res", "seq", None))
    return jax.shard_map(
        functools.partial(body, mesh.shape["seq"], mesh.shape["res"]),
        mesh=mesh,
        in_specs=placed,
        out_specs=(P("res", "seq", None), P("seq", "res", None), P(), P()),
        check_vma=False,
    )
```
